512 devices in a mesh: dp: 8 (over x, core), shard: 64 (over y, z).
Axes of the slice: x: 4, y: 8, z: 8, core: 2. Of those that a mesh axis runs over, the one named last changes fastest.
Arguments:
- queries: bfloat16 [262144, 1024], P(('dp', 'shard')), may hold values from -6 to 6
- query_weight: bfloat16 [1024, 256], replicated, may hold values from -0.1875 to 0.1875
- item_weight: bfloat16 [1024, 256], replicated, may hold values from -0.1875 to 0.1875
- table: bfloat16 [16384, 1024], P('shard'), may hold values from -6 to 6
- queue: bfloat16 [65536, 256], P(('dp', 'shard')), may hold values from -0.0625 to 0.0625
- requests: int32 [32768, 4], P(('dp', 'shard')), may hold values from -1 to 255, as said below
- inverse: int32 [262144], P(('dp', 'shard')), may hold values from 0 to 255, as said below
- write_owner: int32 [1], replicated, may hold values from 0 to 63
Outputs:
- query_update: bfloat16 [1024, 256], replicated
- item_update: bfloat16 [1024, 256], replicated
- new_queue: bfloat16 [65536, 256], P(('dp', 'shard'))
The draws below stay inside these ranges and needn't reach their ends.
Inputs may be any that keep to these rules, and one draw needn't show every extreme that they name: `requests`: in each block an entry is a local row of the owner or -1; entries at and after the block's count are -1, at least one is not; the rows of one block are distinct; every device has a block with exactly 4 rows. `inverse`: every entry names a slot o * 4 + c whose request entry is not -1; every such slot of the device is named by some query.
All inputs are finite; a program needn't handle non-finite values.
Results may differ from the reference program's by a relative error of at most 0.015.
Values may be sent and summed in bfloat16 or wider, within the bound.
A program may use at most 64 MiB of HBM per device.

```python
import math
import jax
import jax.numpy as jnp
from jax import lax

D = 1024
E = 256
Q_DEV = 512
QUEUE_DEV = 128
TABLE_DEV = 256
CAP = 4
FRESH_DEV = 1
TOKENS = 262144
TABLE = 16384
QUEUE = 65536
N_DP = 8
N_SHARD = 64


def request_counts(key):
    count_key, owner_key = jax.random.split(key)
    devices = N_DP * N_SHARD
    counts = jax.random.randint(count_key, (devices, N_SHARD), 1, CAP + 1)
    counts = counts.at[0, 0].set(1)
    full_owner = jax.random.randint(owner_key, (devices, 1), 0, N_SHARD)
    full_owner = full_owner.at[0, 0].set(N_SHARD - 1)
    owner_ids = jnp.arange(N_SHARD, dtype=jnp.int32)[None, :]
    return jnp.where(owner_ids == full_owner, CAP, counts).astype(jnp.int32)


def draw_requests(key, part):
    counts = request_counts(key)
    key = jax.random.fold_in(key, 11)
    base_key, jitter_key = jax.random.split(key)
    devices = N_DP * N_SHARD
    stride = TABLE_DEV // CAP
    base_row = jax.random.randint(base_key, (devices, N_SHARD, 1), 0, TABLE_DEV)
    jitter = jax.random.randint(jitter_key, (devices, N_SHARD, CAP), 0, stride)
    base_row = base_row.at[0, 0, 0].set(TABLE_DEV - 1 - jitter[0, 0, 0])
    slot_place = jnp.arange(CAP, dtype=jnp.int32)[None, None, :]
    table_rows = (base_row + slot_place * stride + jitter) % TABLE_DEV
    marked = jnp.where(slot_place < counts[:, :, None], table_rows, -1)
    return marked.reshape(devices * N_SHARD, CAP).astype(jnp.int32)


def draw_inverse(key, part):
    counts = request_counts(key)
    key = jax.random.fold_in(key, 23)
    pick_key, order_key = jax.random.split(key)
    devices = N_DP * N_SHARD
    used = jnp.sum(counts, axis=1, keepdims=True)
    places = jnp.arange(Q_DEV, dtype=jnp.int32)[None, :]
    extra_pick = jax.random.randint(pick_key, (devices, Q_DEV), 0, N_SHARD * CAP) % used
    chosen = jnp.where(places < used, places, extra_pick)
    block_ends = jnp.cumsum(counts, axis=1)
    owner_of = jnp.sum((chosen[:, :, None] >= block_ends[:, None, :]).astype(jnp.int32), axis=2)
    block_starts = block_ends - counts
    start_of = jnp.take_along_axis(block_starts, owner_of, axis=1)
    slot_ids = owner_of * CAP + chosen - start_of
    order_keys = jax.random.split(order_key, devices)
    query_order = jax.vmap(lambda one_key: jax.random.permutation(one_key, Q_DEV))(order_keys)
    shuffled = jnp.take_along_axis(slot_ids, query_order, axis=1)
    return shuffled.reshape(devices * Q_DEV).astype(jnp.int32)


def shard_levels(key, extent, pieces, smallest, top_value):
    loudness, own = 1.0, jax.random.fold_in(key, 6)
    for dim, parts in pieces:
        draws = jnp.exp(jax.random.uniform(jax.random.fold_in(own, dim), (parts,), jnp.float32, smallest / len(pieces), top_value / len(pieces)))
        loudness = loudness * jnp.repeat(draws, extent[dim] // parts).reshape([-1 if axis == dim else 1 for axis in range(len(extent))])
    return loudness


def scatter_about(own_key, extent, deviation, most, cuts=(), held_as=jnp.bfloat16):
    loudness = shard_levels(own_key, extent, cuts, -0.22, 0.18) if cuts else 1.0
    array = jax.random.normal(own_key, extent, jnp.float32) * deviation * loudness
    return jnp.minimum(jnp.maximum(array, -most), most).astype(held_as)


def setup_inputs(seed: int = 0) -> dict:
    arg_keys = jax.random.split(jax.random.key(seed), 9)
    queries = scatter_about(arg_keys[0], (TOKENS, D), 1.0, 6.0, ((0, 512),))
    query_weight = scatter_about(arg_keys[1], (D, E), D ** -0.5, 0.1875)
    item_weight = scatter_about(arg_keys[2], (D, E), D ** -0.5, 0.1875)
    table = scatter_about(arg_keys[3], (TABLE, D), 1.0, 6.0, ((0, 64),))
    queue = jnp.clip(jax.random.uniform(arg_keys[4], (QUEUE, E), jnp.float32, -0.0625, 0.0625) * shard_levels(arg_keys[4], (QUEUE, E), ((0, 512),), -0.4, 0.0), -0.0625, 0.0625).astype(jnp.bfloat16)
    requests = draw_requests(jax.random.fold_in(arg_keys[8], 71), 0)
    inverse = draw_inverse(jax.random.fold_in(arg_keys[8], 71), 0)
    write_owner = jax.random.randint(arg_keys[7], (1,), 0, N_SHARD).astype(jnp.int32)
    return dict(queries=queries, query_weight=query_weight, item_weight=item_weight, table=table, queue=queue, requests=requests, inverse=inverse, write_owner=write_owner)


LOGIT_SCALE = 50.0
NORM_EPS = 1e-06

def unit_rows(raw_rows):
    sq_total = lax.optimization_barrier(jnp.sum(raw_rows * raw_rows, axis=-1, keepdims=True)) + NORM_EPS
    return (raw_rows * lax.rsqrt(sq_total), sq_total)

def unit_back(raw_rows, sq_total, grad_in):
    inner_dot = lax.optimization_barrier(jnp.sum(raw_rows * grad_in, axis=-1, keepdims=True))
    root_inv = lax.rsqrt(sq_total)
    return grad_in * root_inv - raw_rows * (inner_dot * root_inv / sq_total)

def device_terms(query_block, asked_ids, inverse_block, table, queue_rep, query_weight, item_weight):
    owner_rows = jnp.arange(N_SHARD, dtype=jnp.int32)[:, None] * TABLE_DEV
    table_rows = (owner_rows + jnp.maximum(asked_ids, 0)).reshape(-1)
    fetched = table[table_rows]
    item_raw = jnp.dot(fetched, item_weight, preferred_element_type=jnp.float32).astype(jnp.bfloat16)
    item_wide = item_raw.astype(jnp.float32)
    item_unit, item_total = unit_rows(item_wide)
    item_embed = item_unit.astype(jnp.bfloat16)
    query_raw = jnp.dot(query_block, query_weight, preferred_element_type=jnp.float32)
    query_unit, query_total = unit_rows(query_raw)
    query_embed = query_unit.astype(jnp.bfloat16)
    positive = item_embed[inverse_block]
    pos_logit = LOGIT_SCALE * lax.optimization_barrier(jnp.sum(query_embed.astype(jnp.float32) * positive.astype(jnp.float32), axis=1))
    neg_logit = LOGIT_SCALE * jnp.dot(query_embed, queue_rep.T, preferred_element_type=jnp.float32)
    expos = jnp.exp(neg_logit)
    pos_expo = jnp.exp(pos_logit)
    denom = pos_expo + lax.optimization_barrier(jnp.sum(expos, axis=1))
    weighted = jnp.dot(expos.astype(jnp.bfloat16), queue_rep, preferred_element_type=jnp.float32)
    pos_share = pos_expo / denom
    query_grad = LOGIT_SCALE * (weighted / denom[:, None] + (pos_share - 1.0)[:, None] * positive.astype(jnp.float32))
    pos_grad = LOGIT_SCALE * (pos_share - 1.0)[:, None] * query_embed.astype(jnp.float32)
    item_grad = jax.ops.segment_sum(pos_grad, inverse_block, num_segments=N_SHARD * CAP)
    query_back = unit_back(query_raw, query_total, query_grad).astype(jnp.bfloat16)
    item_back = unit_back(item_wide, item_total, item_grad).astype(jnp.bfloat16)
    query_term = jnp.dot(query_block.T, query_back, preferred_element_type=jnp.float32)
    item_term = jnp.dot(fetched.T, item_back, preferred_element_type=jnp.float32)
    return (query_term, item_term, positive[:FRESH_DEV])

def reference(queries, query_weight, item_weight, table, queue, requests, inverse, write_owner):
    devices = N_DP * N_SHARD
    replica_rows = N_SHARD * QUEUE_DEV
    query_blocks = queries.reshape(devices, Q_DEV, D)
    asked_blocks = requests.reshape(devices, N_SHARD, CAP)
    inverse_blocks = inverse.reshape(devices, Q_DEV)

    def device_step(fold_carry, inputs):
        query_sum, item_sum = fold_carry
        dev_index, query_block, asked_ids, inverse_block = inputs
        replica = dev_index // N_SHARD
        queue_rep = lax.dynamic_slice_in_dim(queue, (replica * replica_rows).astype(jnp.int32), replica_rows, 0)
        query_term, item_term, fresh_embed = device_terms(query_block, asked_ids, inverse_block, table, queue_rep, query_weight, item_weight)
        return ((query_sum + query_term, item_sum + item_term), fresh_embed)
    zero_grad = jnp.zeros((D, E), jnp.float32)
    dev_ids = jnp.arange(devices, dtype=jnp.int32)
    (query_sum, item_sum), fresh_all = lax.scan(device_step, (zero_grad, zero_grad), (dev_ids, query_blocks, asked_blocks, inverse_blocks))
    squares = jnp.sum(query_sum * query_sum) + jnp.sum(item_sum * item_sum)
    factor = jnp.minimum(1.0, math.sqrt(2.0 * D * E) / jnp.sqrt(squares + NORM_EPS))
    query_update = (query_sum * factor).astype(jnp.bfloat16)
    item_update = (item_sum * factor).astype(jnp.bfloat16)
    written = fresh_all.reshape(N_DP, 1, N_SHARD * FRESH_DEV, E)
    blocks = queue.reshape(N_DP, N_SHARD, QUEUE_DEV, E)
    zero_index = jnp.zeros((), jnp.int32)
    blocks = lax.dynamic_update_slice(blocks, written, (zero_index, write_owner[0].astype(jnp.int32), zero_index, zero_index))
    return (query_update, item_update, blocks.reshape(-1, E))
```

```python
import functools
import math

import jax
import jax.numpy as jnp
from jax import lax
from jax.experimental import pallas as pl
from jax.experimental.pallas import tpu as pltpu
from jax.sharding import PartitionSpec as P

SCALE = 50.0
EPS = 1e-06
CAP = 4
BF = jnp.bfloat16
F32 = jnp.float32
LOG2E = math.log2(math.e)
MESH = pl.DeviceIdType.MESH


def dot(a, b, lhs=1, rhs=0):
    return lax.dot_general(a, b, (((lhs,), (rhs,)), ((), ())), preferred_element_type=F32)


def split_dot(a, wide):
    high = wide.astype(BF)
    low = (wide - high.astype(F32)).astype(BF)
    return dot(a, high) + dot(a, low)


def pick(mask):
    return jnp.where(mask, 1.0, 0.0).astype(BF)


def unit_back(raw, total, grad):
    inner = jnp.sum(raw * grad, axis=-1, keepdims=True)
    inv = lax.rsqrt(total)
    return grad * inv - raw * (inner * inv / total)


class Sems:
    def __init__(self, send, recv):
        self.send, self.recv, self.used = send, recv, 0
        self.open = []

    def copy(self, src, dst, device):
        i = self.used
        self.used += 1
        made = pltpu.make_async_remote_copy(
            src_ref=src, dst_ref=dst, send_sem=self.send.at[i], recv_sem=self.recv.at[i],
            device_id=device, device_id_type=MESH,
        )
        self.open.append(made)
        return made


def n_sems(sizes):
    nx, ny, nz, nc = sizes
    y, z, x, c = ny - 1, nz - 1, nx - 1, nc - 1
    gather = y + z + 2 * (y + z)
    items = 2 * (y + z) * 2 + (y + z)
    reduce = 2 * (c + x + y) + z + y + x + c
    return gather + items + reduce


def kernel(sizes, q_ref, qw_ref, iw_ref, t_ref, r_ref, id_ref, inv_ref, outq_ref, outi_ref, fresh_ref,
           buf, qt, tt, traw, qraw, qe, wacc, dacc, mt, ot, iraw, pos,
           id1, id2, id2s, rs1, rr1, rs2, rr2, fs1, fr1, fs2, fr2, bs1, br1, bs2, br2,
           term, sc, rc, sx, rx, sy, ry, zs, rz, fin, send_sem, recv_sem):
    nx, ny, nz, nc = sizes
    ns = ny * nz
    slots = ns * CAP
    d, s = lax.axis_index("dp"), lax.axis_index("shard")
    x, core = lax.div(d, nc), lax.rem(d, nc)
    y, z = lax.div(s, nz), lax.rem(s, nz)
    at_y = lambda p: (d, p * nz + z)
    at_z = lambda p: (d, y * nz + p)
    at_x = lambda p: (p * nc + core, s)
    at_c = lambda p: (x * nc + p, s)
    sems = Sems(send_sem, recv_sem)

    barrier = pltpu.get_barrier_semaphore()
    total = 0
    for at, n, me in ((at_y, ny, y), (at_z, nz, z), (at_x, nx, x), (at_c, nc, core)):
        for k in range(1, n):
            pl.semaphore_signal(barrier, inc=1, device_id=at(lax.rem(me + k, n)), device_id_type=MESH)
            total += 1
    pl.semaphore_wait(barrier, total)

    def exchange(at, n, me, src, dst):
        made = []
        for k in range(1, n):
            p = lax.rem(me + k, n)
            made.append(sems.copy(src(p), dst(me), at(p)))
        for one in made:
            one.start()
        return made

    def arrive(made):
        for one in made:
            one.wait_recv()

    ids_y = exchange(at_y, ny, y, lambda p: id_ref.at[pl.ds(pl.multiple_of(p * nz, nz), nz)], lambda me: id1.at[me])
    half = r_ref.shape[0] // 2
    gather_y = exchange(at_y, ny, y, lambda p: r_ref.at[pl.ds(0, half)], lambda me: buf.at[0, z, me])
    gather_z = exchange(at_z, nz, z, lambda p: r_ref.at[pl.ds(half, half)], lambda me: buf.at[1, y, me])
    id1[y] = id_ref[pl.ds(pl.multiple_of(y * nz, nz), nz), :]
    buf[0, z, y] = r_ref[pl.ds(0, half), :]
    buf[1, y, z] = r_ref[pl.ds(half, half), :]

    traw[...] = dot(t_ref[...], iw_ref[...]).astype(BF)
    raw = dot(q_ref[...], qw_ref[...])
    qraw[...] = raw
    q_total = jnp.sum(raw * raw, axis=-1, keepdims=True) + EPS
    qe[...] = (raw * lax.rsqrt(q_total)).astype(BF)
    wacc[...] = jnp.zeros_like(wacc)
    dacc[...] = jnp.zeros_like(dacc)

    arrive(ids_y)
    id2s[...] = jnp.sum(id1[...], axis=0)
    id2[z] = id2s[...]
    ids_z = exchange(at_z, nz, z, lambda p: id2s, lambda me: id2.at[me])

    arrive(gather_y)
    arrive(gather_z)
    rings = ((at_z, nz, z, ny), (at_y, ny, y, nz))
    messages = {}
    for h, (at, n, me, width) in enumerate(rings):
        for left in (0, 1):
            for i in range(n - 1):
                last = i == n - 2
                away = n // 2 - 1 if last else i // 2
                part = left if last else i % 2
                col = lax.rem(me + (away if left else n - away), n)
                ref = buf.at[h, col, pl.ds(part * (width // 2), width // 2)]
                to = lax.rem(me + (n - 1 if left else 1), n)
                messages[h, left, i] = sems.copy(ref, ref, at(to))

    def go(h, left, i):
        messages[h, left, i].start()

    def attend(h, col, part, width):
        rows = buf[h, col, pl.ds(part * (width // 2), width // 2)]
        keys = rows.reshape(rows.shape[0] * rows.shape[1], rows.shape[2])
        expo = jnp.exp2(dot(qe[...], keys, 1, 1) * (SCALE * LOG2E))
        wacc[...] += dot(expo.astype(BF), keys)
        lanes = dacc.shape[1]
        dacc[...] += sum(expo[:, k : k + lanes] for k in range(0, expo.shape[1], lanes))

    def step(m):
        n = nz
        for h in (0, 1):
            for left in (0, 1):
                messages[h, left, m].wait_recv()
                last = n - 2
                if left and m == n - 3:
                    go(h, left, last)
                elif m + 2 <= last - left:
                    go(h, left, m + 2)

        def body(t, carry):
            h, left = lax.div(t, 2), lax.rem(t, 2)
            me = jnp.where(h == 0, z, y)
            away = m // 2 + 1
            col = lax.rem(jnp.where(left == 1, me + away, me + n - away), n)
            part = left if m == n - 2 else m % 2
            attend(h, col, part, n)
            return carry

        lax.fori_loop(0, 4, body, 0)

    for h in (0, 1):
        for left in (0, 1):
            for i in range(min(2, nz - 1)):
                go(h, left, i)

    arrive(ids_z)
    mine = lax.broadcasted_iota(jnp.int32, (nz, slots), 0) == z
    asked = jnp.sum(jnp.where(mine, jnp.sum(id2[...], axis=0), 0), axis=0, keepdims=True)
    mt[...] = pick(lax.broadcasted_iota(jnp.int32, mt.shape, 0) == asked)
    rs1[...] = dot(mt[...], traw[...], 0, 0).astype(BF).reshape(rs1.shape)
    rr1[y] = rs1[y]
    rows_y = exchange(at_y, ny, y, lambda p: rs1.at[p], lambda me: rr1.at[me])

    def own_body(t, carry):
        h = lax.div(t, 2)
        attend(h, jnp.where(h == 0, z, y), lax.rem(t, 2), nz)
        return carry

    lax.fori_loop(0, 4, own_body, 0)
    qt[...] = q_ref[...].T
    if nz - 1 > 0:
        step(0)

    def slot_of(i):
        zo, yo, c = i // (ny * CAP), (i // CAP) % ny, i % CAP
        return (yo * nz + zo) * CAP + c

    square = (slots, slots)
    arrive(rows_y)
    order = pick(lax.broadcasted_iota(jnp.int32, square, 1) == slot_of(lax.broadcasted_iota(jnp.int32, square, 0)))
    rs2[...] = dot(order, rr1[...].reshape(slots, -1)).astype(BF).reshape(rs2.shape)
    rr2[z] = rs2[z]
    rows_z = exchange(at_z, nz, z, lambda p: rs2.at[p], lambda me: rr2.at[me])
    tt[...] = t_ref[...].T
    for m in range(1, min(3, nz - 1)):
        step(m)

    arrive(rows_z)
    item = rr2[...].reshape(slots, -1).astype(F32)
    iraw[...] = item
    i_total = jnp.sum(item * item, axis=-1, keepdims=True) + EPS
    embed = (item * lax.rsqrt(i_total)).astype(BF)
    slot_rows = slot_of(lax.broadcasted_iota(jnp.int32, ot.shape, 0))
    ot[...] = pick(slot_rows == inv_ref[...])
    pos[...] = dot(ot[...], embed, 0, 0)
    first = jnp.broadcast_to(pos[0:1, :], fs1.shape)
    fs1[...] = jnp.where(lax.broadcasted_iota(jnp.int32, fs1.shape, 0) == y, first, 0.0).astype(BF)
    fr1[y] = fs1[...]
    fresh_y = exchange(at_y, ny, y, lambda p: fs1, lambda me: fr1.at[me])
    for m in range(3, min(5, nz - 1)):
        step(m)
    arrive(fresh_y)
    fs2[...] = jnp.sum(fr1[...].astype(F32), axis=0).astype(BF)
    fr2[z] = fs2[...]
    fresh_z = exchange(at_z, nz, z, lambda p: fs2, lambda me: fr2.at[me])
    for m in range(5, nz - 1):
        step(m)
    arrive(fresh_z)
    fshape = (ns, nz * fs2.shape[0])
    want = lax.broadcasted_iota(jnp.int32, fshape, 0)
    place = (want % nz) * fs2.shape[0] + want // nz
    fresh_ref[...] = dot(pick(lax.broadcasted_iota(jnp.int32, fshape, 1) == place),
                         fr2[...].reshape(fshape[1], -1)).astype(BF)

    raw = qraw[...]
    q_total = jnp.sum(raw * raw, axis=-1, keepdims=True) + EPS
    embed = qe[...].astype(F32)
    positive = pos[...]
    pos_expo = jnp.exp(SCALE * jnp.sum(embed * positive, axis=1, keepdims=True))
    denom = pos_expo + jnp.sum(dacc[...], axis=1, keepdims=True)
    less = pos_expo / denom - 1.0
    item_grad = split_dot(ot[...], (SCALE * less) * embed)
    item = iraw[...]
    i_total = jnp.sum(item * item, axis=-1, keepdims=True) + EPS
    bs1[...] = unit_back(item, i_total, item_grad).astype(BF).reshape(bs1.shape)
    br1[z] = bs1[z]
    back_z = exchange(at_z, nz, z, lambda p: bs1.at[p], lambda me: br1.at[me])
    query_grad = SCALE * (wacc[...] / denom + less * positive)
    query_back = unit_back(raw, q_total, query_grad).astype(BF)

    part = term.shape[1] // nc

    def core_send(a):
        if nc == 1:
            return []
        other = pl.multiple_of((1 - core) * part, part)
        sc[a] = term[a, pl.ds(other, part), :].astype(BF)
        return exchange(at_c, nc, core, lambda p: sc.at[a], lambda me: rc.at[a])

    def core_sum(a):
        own = term[a, pl.ds(pl.multiple_of(core * part, part), part), :]
        return own + rc[a].astype(F32) if nc > 1 else own

    px, py = part // nx, part // nx // ny

    def ring_send(value, n, me, at, src, dst, a):
        src[a] = value.astype(BF).reshape(src.shape[1:])
        return exchange(at, n, me, lambda p: src.at[a, p], lambda me: dst.at[a, me])

    def ring_sum(value_ref, recv, n, me, a):
        total = value_ref
        for k in range(1, n):
            total = total + recv[a, lax.rem(me + k, n)].astype(F32)
        return total

    term[0] = dot(qt[...], query_back)
    c_q = core_send(0)
    arrive(back_z)
    order = pick(lax.broadcasted_iota(jnp.int32, square, 0) == slot_of(lax.broadcasted_iota(jnp.int32, square, 1)))
    bs2[...] = dot(order, br1[...].reshape(slots, -1)).astype(BF).reshape(bs2.shape)
    br2[y] = bs2[y]
    back_y = exchange(at_y, ny, y, lambda p: bs2.at[p], lambda me: br2.at[me])

    def x_send(a):
        value = core_sum(a)
        term[a, pl.ds(0, part), :] = value
        return ring_send(value, nx, x, at_x, sx, rx, a)

    def y_send(a):
        own = term[a, pl.ds(pl.multiple_of(x * px, px), px), :]
        value = ring_sum(own, rx, nx, x, a)
        term[a, pl.ds(0, px), :] = value
        return ring_send(value, ny, y, at_y, sy, ry, a)

    def z_value(a):
        own = term[a, pl.ds(pl.multiple_of(y * py, py), py), :]
        return ring_sum(own, ry, ny, y, a)

    arrive(c_q)
    x_q = x_send(0)
    arrive(back_y)
    owned = dot(mt[...], br2[...].reshape(slots, -1))
    term[1] = split_dot(tt[...], owned)
    c_i = core_send(1)
    arrive(x_q)
    y_q = y_send(0)
    arrive(c_i)
    x_i = x_send(1)
    arrive(y_q)
    zs[0] = z_value(0).astype(BF)
    arrive(x_i)
    y_i = y_send(1)
    arrive(y_i)
    zs[1] = z_value(1).astype(BF)
    rz[z] = zs[...]
    arrive(exchange(at_z, nz, z, lambda p: zs, lambda me: rz.at[me]))
    fin[core, x, y] = jnp.sum(rz[...].astype(F32), axis=0).astype(BF)
    mine = lambda me: fin.at[core, x, y]
    arrive(exchange(at_y, ny, y, lambda p: fin.at[core, x, y], mine))
    arrive(exchange(at_x, nx, x, lambda p: fin.at[core, x], lambda me: fin.at[core, x]))
    arrive(exchange(at_c, nc, core, lambda p: fin.at[core], lambda me: fin.at[core]))

    sums = fin[...].astype(F32)
    squares = jnp.sum(jnp.sum(sums * sums, axis=(0, 1, 2, 3)), keepdims=True)
    limit = math.sqrt(2.0 * outq_ref.shape[0] * outq_ref.shape[1])
    factor = jnp.minimum(1.0, limit / jnp.sqrt(squares + EPS))
    outq_ref[...] = (sums[:, :, :, 0].reshape(outq_ref.shape) * factor).astype(BF)
    outi_ref[...] = (sums[:, :, :, 1].reshape(outi_ref.shape) * factor).astype(BF)
    for one in sems.open:
        one.wait_send()


def per_device(sizes, queries, query_weight, item_weight, table, queue, requests, inverse, write_owner):
    nx, ny, nz, nc = sizes
    ns = ny * nz
    slots = ns * CAP
    width, embed = query_weight.shape
    n_q, n_t = queries.shape[0], table.shape[0]
    n_r = queue.shape[0] // 2
    s = lax.axis_index("shard")
    lane = jnp.arange(slots, dtype=jnp.int32)[None, :]
    ids = jnp.where(lane // CAP == s, jnp.tile(jnp.maximum(requests, 0), (1, ns)), 0)
    part = width // nc
    px, py = part // nx, part // nx // ny
    vm = lambda shape, dtype: pltpu.VMEM(shape, dtype)
    zrows, yrows = ny * CAP, nz * CAP
    scratch = [
        vm((2, nz, ny, n_r, embed), BF),
        vm((width, n_q), BF),
        vm((width, n_t), BF),
        vm((n_t, embed), BF),
        vm((n_q, embed), F32),
        vm((n_q, embed), BF),
        vm((n_q, embed), F32),
        vm((n_q, 128), F32),
        vm((n_t, slots), BF),
        vm((slots, n_q), BF),
        vm((slots, embed), F32),
        vm((n_q, embed), F32),
        vm((ny, nz, slots), jnp.int32),
        vm((nz, nz, slots), jnp.int32),
        vm((nz, slots), jnp.int32),
        vm((ny, yrows, embed), BF),
        vm((ny, yrows, embed), BF),
        vm((nz, zrows, embed), BF),
        vm((nz, zrows, embed), BF),
        vm((16, embed), BF),
        vm((ny, 16, embed), BF),
        vm((16, embed), BF),
        vm((nz, 16, embed), BF),
        vm((nz, zrows, embed), BF),
        vm((nz, zrows, embed), BF),
        vm((ny, yrows, embed), BF),
        vm((ny, yrows, embed), BF),
        vm((2, width, embed), F32),
        vm((2, part, embed), BF),
        vm((2, part, embed), BF),
        vm((2, nx, px, embed), BF),
        vm((2, nx, px, embed), BF),
        vm((2, ny, py, embed), BF),
        vm((2, ny, py, embed), BF),
        vm((2, py, embed), BF),
        vm((nz, 2, py, embed), BF),
        vm((nc, nx, ny, 2, py, embed), BF),
        pltpu.SemaphoreType.DMA((n_sems(sizes),)),
        pltpu.SemaphoreType.DMA((n_sems(sizes),)),
    ]
    full = pl.BlockSpec(memory_space=pltpu.VMEM)
    out_q, out_i, fresh = pl.pallas_call(
        functools.partial(kernel, sizes),
        out_shape=[
            jax.ShapeDtypeStruct((width, embed), BF),
            jax.ShapeDtypeStruct((width, embed), BF),
            jax.ShapeDtypeStruct((ns, embed), BF),
        ],
        in_specs=[full] * 7,
        out_specs=[full] * 3,
        scratch_shapes=scratch,
        compiler_params=pltpu.CompilerParams(
            collective_id=0, has_side_effects=True, vmem_limit_bytes=48 * 2**20
        ),
        name="step",
    )(queries, query_weight, item_weight, table, queue, ids, inverse.reshape(1, n_q))
    updated = jnp.concatenate([fresh, queue[ns:]], axis=0)
    new_queue = jnp.where(s == write_owner[0], updated, queue)
    return out_q, out_i, new_queue


def solution(mesh, sizes=(4, 8, 8, 2)):
    placed = (
        P(("dp", "shard"), None),
        P(),
        P(),
        P("shard", None),
        P(("dp", "shard"), None),
        P(("dp", "shard"), None),
        P(("dp", "shard")),
        P(),
    )
    return jax.shard_map(
        functools.partial(per_device, sizes),
        mesh=mesh,
        in_specs=placed,
        out_specs=(P(), P(), P(("dp", "shard"), None)),
        check_vma=False,
    )
```

```python
import functools
import math

import jax
import jax.numpy as jnp
from jax import lax
from jax.experimental import pallas as pl
from jax.experimental.pallas import tpu as pltpu
from jax.sharding import PartitionSpec as P

SCALE = 50.0
EPS = 1e-06
CAP = 4
BF = jnp.bfloat16
F32 = jnp.float32
LOG2E = math.log2(math.e)
MESH = pl.DeviceIdType.MESH


def dot(a, b, lhs=1, rhs=0):
    return lax.dot_general(a, b, (((lhs,), (rhs,)), ((), ())), preferred_element_type=F32)


def split_dot(a, wide):
    high = wide.astype(BF)
    low = (wide - high.astype(F32)).astype(BF)
    return dot(a, high) + dot(a, low)


def pick(mask):
    return jnp.where(mask, 1.0, 0.0).astype(BF)


def unit_back(raw, total, grad):
    inner = jnp.sum(raw * grad, axis=-1, keepdims=True)
    inv = lax.rsqrt(total)
    return grad * inv - raw * (inner * inv / total)


class Link:
    def __init__(self, made):
        self.made, self.started, self.arrived = made, False, False

    def start(self):
        self.started = True
        self.made.start()

    def wait_recv(self):
        self.arrived = True
        self.made.wait_recv()


class Sems:
    def __init__(self, send, recv):
        self.send, self.recv, self.used = send, recv, 0
        self.open = []

    def copy(self, src, dst, device):
        i = self.used
        self.used += 1
        made = Link(pltpu.make_async_remote_copy(
            src_ref=src, dst_ref=dst, send_sem=self.send.at[i], recv_sem=self.recv.at[i],
            device_id=device, device_id_type=MESH,
        ))
        self.open.append(made)
        return made

    def finish(self):
        for one in self.open:
            if one.started and not one.arrived:
                one.wait_recv()
        for one in self.open:
            if one.started:
                one.made.wait_send()


def n_sems(sizes):
    nx, ny, nz, nc = sizes
    y, z, x, c = ny - 1, nz - 1, nx - 1, nc - 1
    gather = 2 * y + 2 * y * (ny // 2 + 1)
    items = 2 * (y + z) * 2 + (y + z)
    reduce = 2 * (c + x + y) + z + y + (ny // 2 + 1) * (x + c * nx)
    return gather + items + reduce


def kernel(sizes, q_hbm, qw_hbm, iw_hbm, t_hbm, r_ref, req_ref, inv_ref, fin, fresh_ref,
           q_ref, qw_ref, iw_ref, t_ref, local_sem, id_ref, buf, qt, tt, traw, qraw, qe, wacc, dacc, mt, ot, iraw, pos, pos_expo,
           id1, id2, id2s, rs1, rr1, rs2, rr2, fs1, fr1, fs2, fr2, bs1, br1, bs2, br2,
           term, sc, rc, sx, rx, sy, ry, zs, rz, send_sem, recv_sem):
    nx, ny, nz, nc = sizes
    ns = ny * nz
    slots = ns * CAP
    d, s = lax.axis_index("dp"), lax.axis_index("shard")
    x, core = lax.div(d, nc), lax.rem(d, nc)
    y, z = lax.div(s, nz), lax.rem(s, nz)
    at_y = lambda p: (d, p * nz + z)
    at_z = lambda p: (d, y * nz + p)
    at_x = lambda p: (p * nc + core, s)
    at_c = lambda p: (x * nc + p, s)
    sems = Sems(send_sem, recv_sem)
    local = [
        pltpu.make_async_copy(src, dst, local_sem.at[i])
        for i, (src, dst) in enumerate(((t_hbm, t_ref), (iw_hbm, iw_ref), (q_hbm, q_ref), (qw_hbm, qw_ref)))
    ]
    for one in local:
        one.start()
    lane = lax.broadcasted_iota(jnp.int32, (CAP, slots), 1)
    spot = lax.broadcasted_iota(jnp.int32, (CAP, slots), 0)
    asks = jnp.maximum(req_ref[...], 0).astype(F32)
    id_ref[...] = dot(asks, jnp.where(lane == s * CAP + spot, 1.0, 0.0), 0, 0).astype(jnp.int32)

    barrier = pltpu.get_barrier_semaphore()
    total = 0
    for at, n, me in ((at_y, ny, y), (at_z, nz, z), (at_x, nx, x), (at_c, nc, core)):
        for k in range(1, n):
            pl.semaphore_signal(barrier, inc=1, device_id=at(lax.rem(me + k, n)), device_id_type=MESH)
            total += 1
    pl.semaphore_wait(barrier, total)

    def exchange(at, n, me, src, dst):
        made = []
        for k in range(1, n):
            p = lax.rem(me + k, n)
            made.append(sems.copy(src(p), dst(me), at(p)))
        for one in made:
            one.start()
        return made

    def arrive(made):
        for one in made:
            one.wait_recv()

    n = ny
    half = r_ref.shape[0] // 2
    far = n // 2
    pieces = [(0, 1)] + [(2 * k - 1, 2) for k in range(1, far)] + [(n - 1, 1)]
    rightward = {0, far} | set(range(1, n // 4))

    def slot(offset):
        return n - 1 if abs(offset) == far else 2 * offset - 1 if offset > 0 else -2 * offset

    first, second = {}, {}
    axes = (((at_y, y), (at_z, z)), ((at_z, z), (at_y, y)))
    for h in (0, 1):
        (at1, me1), (at2, me2) = axes[h]
        for left in (0, 1):
            turn = 1 if left else -1
            hop = n - 1 if left else 1
            to2 = at2(lax.rem(me2 + hop, n))
            for k in range(1, far + 1):
                if k < far or left == h:
                    src, hops = (r_ref.at[pl.ds(h * half, half)], k) if k < 3 else (buf.at[h, 0, slot(turn * 2)], k - 2)
                    to1 = at1(lax.rem(me1 + hops * hop, n))
                    first[h, left, k] = sems.copy(src, buf.at[h, 0, slot(turn * k)], to1)
                for p, (begin, size) in enumerate(pieces):
                    if k < far or (p in rightward) == (left == 0):
                        at = pl.ds(begin, size)
                        second[h, left, k, p] = sems.copy(
                            buf.at[h, slot(turn * (k - 1)), at], buf.at[h, slot(turn * k), at], to2)

    streams = [(h, left) for h in (0, 1) for left in (0, 1)]

    def send_first(*distances):
        for k in distances:
            for h, left in streams:
                if (h, left, k) in first:
                    first[h, left, k].start()

    def have_first(*distances):
        for k in distances:
            for h, left in streams:
                if (h, left, k) in first:
                    first[h, left, k].wait_recv()

    def send_column(*which):
        for p in which:
            for h, left in streams:
                if (h, left, 1, p) in second:
                    second[h, left, 1, p].start()

    def ring(k, *which):
        for p in which:
            for h, left in streams:
                if (h, left, k, p) in second:
                    second[h, left, k, p].wait_recv()
                    if (h, left, k + 1, p) in second:
                        second[h, left, k + 1, p].start()

    attended = set()

    def attend(h, offset):
        if abs(offset) > far or (h, slot(offset)) in attended:
            return
        col = slot(offset)
        attended.add((h, col))
        sub = n // 2

        def body(t, carry):
            rows = buf[h, col, pl.ds(t * sub, sub)]
            keys = rows.reshape(sub * half, rows.shape[2])
            expo = jnp.exp2(dot(qe[...], keys, 1, 1) * (SCALE * LOG2E))
            wacc[...] += dot(expo.astype(BF), keys)
            lanes = dacc.shape[1]
            dacc[...] += sum(expo[:, k : k + lanes] for k in range(0, expo.shape[1], lanes))
            return carry

        lax.fori_loop(0, 2, body, 0)

    def slot_of(i):
        zo, yo, c = i // (ny * CAP), (i // CAP) % ny, i % CAP
        return (yo * nz + zo) * CAP + c

    square = (slots, slots)
    send_first(1, 2)
    ids_y = exchange(at_y, ny, y, lambda p: id_ref.at[pl.ds(pl.multiple_of(p * nz, nz), nz)], lambda me: id1.at[me])
    buf[0, 0, 0] = r_ref[pl.ds(0, half), :]
    buf[1, 0, 0] = r_ref[pl.ds(half, half), :]
    send_column(0)
    id1[y] = id_ref[pl.ds(pl.multiple_of(y * nz, nz), nz), :]
    wacc[...] = jnp.zeros_like(wacc)
    dacc[...] = jnp.zeros_like(dacc)
    local[0].wait()
    local[1].wait()
    traw[...] = dot(t_ref[...], iw_ref[...]).astype(BF)
    have_first(1, 2)
    send_first(3, 4)
    send_column(1, 2)
    ring(1, 0)
    local[2].wait()
    local[3].wait()
    raw = dot(q_ref[...], qw_ref[...])
    qraw[...] = raw
    q_total = jnp.sum(raw * raw, axis=-1, keepdims=True) + EPS
    qe[...] = (raw * lax.rsqrt(q_total)).astype(BF)
    arrive(ids_y)
    id2s[...] = jnp.sum(id1[...], axis=0)
    id2[z] = id2s[...]
    ids_z = exchange(at_z, nz, z, lambda p: id2s, lambda me: id2.at[me])
    have_first(3, 4)
    send_column(3, 4)
    ring(1, 1)
    qt[...] = q_ref[...].T
    ring(1, 2)

    arrive(ids_z)
    mine = lax.broadcasted_iota(jnp.int32, (nz, slots), 0) == z
    asked = jnp.sum(jnp.where(mine, jnp.sum(id2[...], axis=0), 0), axis=0, keepdims=True)
    mt[...] = pick(lax.broadcasted_iota(jnp.int32, mt.shape, 0) == asked)
    rs1[...] = dot(mt[...], traw[...], 0, 0).astype(BF).reshape(rs1.shape)
    rr1[y] = rs1[y]
    rows_y = exchange(at_y, ny, y, lambda p: rs1.at[p], lambda me: rr1.at[me])
    ring(1, 3)
    attend(0, 0)
    ring(1, 4)
    attend(1, 0)
    ring(2, 0)
    attend(0, -1)
    ring(2, 1)
    attend(1, -1)
    ring(2, 2)
    attend(0, 1)
    ring(2, 3)
    attend(1, 1)
    ring(2, 4)
    arrive(rows_y)
    order = pick(lax.broadcasted_iota(jnp.int32, square, 1) == slot_of(lax.broadcasted_iota(jnp.int32, square, 0)))
    rs2[...] = dot(order, rr1[...].reshape(slots, -1)).astype(BF).reshape(rs2.shape)
    rr2[z] = rs2[z]
    rows_z = exchange(at_z, nz, z, lambda p: rs2.at[p], lambda me: rr2.at[me])
    ring(3, 0)
    attend(0, -2)
    ring(3, 1)
    attend(1, -2)
    ring(3, 2)
    attend(0, 2)
    ring(3, 3)
    attend(1, 2)
    ring(3, 4)
    tt[...] = t_ref[...].T

    arrive(rows_z)
    item = rr2[...].reshape(slots, -1).astype(F32)
    iraw[...] = item
    i_total = jnp.sum(item * item, axis=-1, keepdims=True) + EPS
    embed = (item * lax.rsqrt(i_total)).astype(BF)
    slot_rows = slot_of(lax.broadcasted_iota(jnp.int32, ot.shape, 0))
    ot[...] = pick(slot_rows == inv_ref[...])
    pos[...] = dot(ot[...], embed, 0, 0)
    pos_expo[...] = jnp.exp(SCALE * jnp.sum(qe[...].astype(F32) * pos[...], axis=1, keepdims=True))
    head = jnp.broadcast_to(pos[0:1, :], fs1.shape)
    fs1[...] = jnp.where(lax.broadcasted_iota(jnp.int32, fs1.shape, 0) == y, head, 0.0).astype(BF)
    fr1[y] = fs1[...]
    fresh_y = exchange(at_y, ny, y, lambda p: fs1, lambda me: fr1.at[me])
    ring(4, 0)
    attend(0, -3)
    ring(4, 1)
    attend(1, -3)
    ring(4, 2)
    attend(0, 3)
    ring(4, 3)
    attend(1, 3)
    ring(4, 4)
    attend(0, -4)
    attend(1, -4)

    raw = qraw[...]
    q_total = jnp.sum(raw * raw, axis=-1, keepdims=True) + EPS
    embed = qe[...].astype(F32)
    positive = pos[...]
    denom = pos_expo[...] + jnp.sum(dacc[...], axis=1, keepdims=True)
    less = pos_expo[...] / denom - 1.0
    item_grad = split_dot(ot[...], (SCALE * less) * embed)
    item = iraw[...]
    i_total = jnp.sum(item * item, axis=-1, keepdims=True) + EPS
    bs1[...] = unit_back(item, i_total, item_grad).astype(BF).reshape(bs1.shape)
    br1[z] = bs1[z]
    back_z = exchange(at_z, nz, z, lambda p: bs1.at[p], lambda me: br1.at[me])
    query_grad = SCALE * (wacc[...] / denom + less * positive)
    query_back = unit_back(raw, q_total, query_grad).astype(BF)

    part = term.shape[1] // nc

    def core_send(a):
        if nc == 1:
            return []
        other = pl.multiple_of((1 - core) * part, part)
        sc[a] = term[a, pl.ds(other, part), :].astype(BF)
        return exchange(at_c, nc, core, lambda p: sc.at[a], lambda me: rc.at[a])

    def core_sum(a):
        own = term[a, pl.ds(pl.multiple_of(core * part, part), part), :]
        return own + rc[a].astype(F32) if nc > 1 else own

    px, py = part // nx, part // nx // ny

    def ring_send(value, n, me, at, src, dst, a):
        src[a] = value.astype(BF).reshape(src.shape[1:])
        return exchange(at, n, me, lambda p: src.at[a, p], lambda me: dst.at[a, me])

    def ring_sum(value_ref, recv, n, me, a):
        total = value_ref
        for k in range(1, n):
            total = total + recv[a, lax.rem(me + k, n)].astype(F32)
        return total

    arrive(fresh_y)
    fs2[...] = jnp.sum(fr1[...].astype(F32), axis=0).astype(BF)
    fr2[z] = fs2[...]
    fresh_z = exchange(at_z, nz, z, lambda p: fs2, lambda me: fr2.at[me])

    term[0] = dot(qt[...], query_back)
    c_q = core_send(0)
    arrive(back_z)
    order = pick(lax.broadcasted_iota(jnp.int32, square, 0) == slot_of(lax.broadcasted_iota(jnp.int32, square, 1)))
    bs2[...] = dot(order, br1[...].reshape(slots, -1)).astype(BF).reshape(bs2.shape)
    br2[y] = bs2[y]
    back_y = exchange(at_y, ny, y, lambda p: bs2.at[p], lambda me: br2.at[me])

    def x_send(a):
        value = core_sum(a)
        term[a, pl.ds(0, part), :] = value
        return ring_send(value, nx, x, at_x, sx, rx, a)

    def y_send(a):
        own = term[a, pl.ds(pl.multiple_of(x * px, px), px), :]
        value = ring_sum(own, rx, nx, x, a)
        term[a, pl.ds(0, px), :] = value
        return ring_send(value, ny, y, at_y, sy, ry, a)

    def z_value(a):
        own = term[a, pl.ds(pl.multiple_of(y * py, py), py), :]
        return ring_sum(own, ry, ny, y, a)

    arrive(c_q)
    x_q = x_send(0)
    arrive(back_y)
    owned = dot(mt[...], br2[...].reshape(slots, -1))
    term[1] = split_dot(tt[...], owned)
    c_i = core_send(1)
    arrive(x_q)
    y_q = y_send(0)
    arrive(c_i)
    x_i = x_send(1)
    arrive(y_q)
    zs[0] = z_value(0).astype(BF)
    arrive(x_i)
    y_i = y_send(1)
    arrive(y_i)
    zs[1] = z_value(1).astype(BF)
    rz[z] = zs[...]
    arrive(exchange(at_z, nz, z, lambda p: zs, lambda me: rz.at[me]))
    fin[core, x, 0] = jnp.sum(rz[...].astype(F32), axis=0).astype(BF)
    groups = [(p,) + piece for p, piece in enumerate(pieces)]
    along_y = {}
    for k in range(1, ny):
        offset = ny - k if ny - k <= far else -k
        along_y[k] = sems.copy(fin.at[core, x, 0], fin.at[core, x, slot(offset)], at_y(lax.rem(y + k, ny)))
        along_y[k].start()

    to_core = []

    def hand_over(xx, begin, size):
        if nc > 1:
            ref = fin.at[core, xx, pl.ds(begin, size)]
            to_core.append(sems.copy(ref, ref, at_c(1 - core)))
            to_core[-1].start()

    along_x = {}
    for p, begin, size in groups:
        for k in sorted({p, ny - p}) if p else ():
            along_y[k].wait_recv()
        ref = fin.at[core, x, pl.ds(begin, size)]
        for k in range(1, nx):
            along_x[p, k] = sems.copy(ref, ref, at_x(lax.rem(x + k, nx)))
            along_x[p, k].start()
        hand_over(x, begin, size)
    arrive(fresh_z)
    fshape = (ns, nz * fs2.shape[0])
    want = lax.broadcasted_iota(jnp.int32, fshape, 0)
    place = (want % nz) * fs2.shape[0] + want // nz
    fresh_ref[...] = dot(pick(lax.broadcasted_iota(jnp.int32, fshape, 1) == place),
                         fr2[...].reshape(fshape[1], -1)).astype(BF)
    for p, begin, size in groups:
        for k in range(1, nx):
            along_x[p, k].wait_recv()
            hand_over(lax.rem(x + nx - k, nx), begin, size)
    arrive(to_core)

    sems.finish()


def clip(nz, sums_ref, fresh_ref, queue_ref, owner_ref, outq, outi, outn, sq, si, sn, sem):
    s = lax.axis_index("shard")
    ny = sums_ref.shape[2]
    y = lax.div(s, nz)
    ns = fresh_ref.shape[0]
    mine = owner_ref[0] == s
    sn[pl.ds(0, ns), :] = jnp.where(mine, fresh_ref[...], queue_ref[pl.ds(0, ns), :])
    sn[pl.ds(ns, sn.shape[0] - ns), :] = queue_ref[pl.ds(ns, sn.shape[0] - ns), :]
    made = [pltpu.make_async_copy(src, dst, sem.at[i]) for i, (src, dst) in enumerate(((sn, outn), (sq, outq), (si, outi)))]
    made[0].start()
    sums = sums_ref[...].astype(F32)
    squares = jnp.sum(jnp.sum(sums * sums, axis=(0, 1, 2, 3)), keepdims=True)
    count = math.prod(sums_ref.shape)
    factor = jnp.minimum(1.0, math.sqrt(count) / jnp.sqrt(squares + EPS))
    for a, out in enumerate((sq, si)):
        for row in range(ny):
            ahead = lax.rem(row - y + ny, ny)
            at = jnp.where(ahead == 0, 0, jnp.where(ahead < ny // 2, 2 * ahead - 1, 2 * (ny - ahead)))
            at = jnp.where(ahead == ny // 2, ny - 1, at)
            out[:, :, row] = (sums_ref[:, :, at, a].astype(F32) * factor).astype(BF)
        made[1 + a].start()
    for one in made:
        one.wait()


def per_device(sizes, queries, query_weight, item_weight, table, queue, requests, inverse, write_owner):
    nx, ny, nz, nc = sizes
    ns = ny * nz
    slots = ns * CAP
    width, embed = query_weight.shape
    n_q, n_t = queries.shape[0], table.shape[0]
    n_r = queue.shape[0] // 2
    s = lax.axis_index("shard")
    part = width // nc
    px, py = part // nx, part // nx // ny
    vm = lambda shape, dtype: pltpu.VMEM(shape, dtype)
    zrows, yrows = ny * CAP, nz * CAP
    scratch = [
        vm(queries.shape, BF),
        vm(query_weight.shape, BF),
        vm(item_weight.shape, BF),
        vm(table.shape, BF),
        pltpu.SemaphoreType.DMA((4,)),
        vm((ns, slots), jnp.int32),
        vm((2, nz, ny, n_r, embed), BF),
        vm((width, n_q), BF),
        vm((width, n_t), BF),
        vm((n_t, embed), BF),
        vm((n_q, embed), F32),
        vm((n_q, embed), BF),
        vm((n_q, embed), F32),
        vm((n_q, 128), F32),
        vm((n_t, slots), BF),
        vm((slots, n_q), BF),
        vm((slots, embed), F32),
        vm((n_q, embed), F32),
        vm((n_q, 1), F32),
        vm((ny, nz, slots), jnp.int32),
        vm((nz, nz, slots), jnp.int32),
        vm((nz, slots), jnp.int32),
        vm((ny, yrows, embed), BF),
        vm((ny, yrows, embed), BF),
        vm((nz, zrows, embed), BF),
        vm((nz, zrows, embed), BF),
        vm((16, embed), BF),
        vm((ny, 16, embed), BF),
        vm((16, embed), BF),
        vm((nz, 16, embed), BF),
        vm((nz, zrows, embed), BF),
        vm((nz, zrows, embed), BF),
        vm((ny, yrows, embed), BF),
        vm((ny, yrows, embed), BF),
        vm((2, width, embed), F32),
        vm((2, part, embed), BF),
        vm((2, part, embed), BF),
        vm((2, nx, px, embed), BF),
        vm((2, nx, px, embed), BF),
        vm((2, ny, py, embed), BF),
        vm((2, ny, py, embed), BF),
        vm((2, py, embed), BF),
        vm((nz, 2, py, embed), BF),
        pltpu.SemaphoreType.DMA((n_sems(sizes),)),
        pltpu.SemaphoreType.DMA((n_sems(sizes),)),
    ]
    full = pl.BlockSpec(memory_space=pltpu.VMEM)
    far = pl.BlockSpec(memory_space=pl.ANY)
    sums, fresh = pl.pallas_call(
        functools.partial(kernel, sizes),
        out_shape=[
            jax.ShapeDtypeStruct((nc, nx, ny, 2, py, embed), BF),
            jax.ShapeDtypeStruct((ns, embed), BF),
        ],
        in_specs=[far] * 4 + [full] * 3,
        out_specs=[full] * 2,
        scratch_shapes=scratch,
        compiler_params=pltpu.CompilerParams(
            collective_id=0, has_side_effects=True, vmem_limit_bytes=56 * 2**20
        ),
        name="step",
    )(queries, query_weight, item_weight, table, queue, requests.T, inverse.reshape(1, n_q))
    laid = (nc, nx, ny, py, embed)
    out_q, out_i, new_queue = pl.pallas_call(
        functools.partial(clip, nz),
        out_shape=[
            jax.ShapeDtypeStruct(laid, BF),
            jax.ShapeDtypeStruct(laid, BF),
            jax.ShapeDtypeStruct(queue.shape, BF),
        ],
        in_specs=[full] * 3 + [pl.BlockSpec(memory_space=pltpu.SMEM)],
        out_specs=[far] * 3,
        scratch_shapes=[
            vm(laid, BF),
            vm(laid, BF),
            vm(queue.shape, BF),
            pltpu.SemaphoreType.DMA((3,)),
        ],
        name="clip",
    )(sums, fresh, queue, write_owner)
    return out_q.reshape(width, embed), out_i.reshape(width, embed), new_queue


def solution(mesh, sizes=(4, 8, 8, 2)):
    placed = (
        P(("dp", "shard"), None),
        P(),
        P(),
        P("shard", None),
        P(("dp", "shard"), None),
        P(("dp", "shard"), None),
        P(("dp", "shard")),
        P(),
    )
    return jax.shard_map(
        functools.partial(per_device, sizes),
        mesh=mesh,
        in_specs=placed,
        out_specs=(P(), P(), P(("dp", "shard"), None)),
        check_vma=False,
    )
```

```python
import functools
import math

import jax
import jax.numpy as jnp
from jax import lax
from jax.experimental import pallas as pl
from jax.experimental.pallas import tpu as pltpu
from jax.sharding import PartitionSpec as P

SCALE = 50.0
EPS = 1e-06
CAP = 4
BF = jnp.bfloat16
F32 = jnp.float32
LOG2E = math.log2(math.e)
MESH = pl.DeviceIdType.MESH


def dot(a, b, lhs=1, rhs=0):
    return lax.dot_general(a, b, (((lhs,), (rhs,)), ((), ())), preferred_element_type=F32)


def split_dot(a, wide):
    high = wide.astype(BF)
    low = (wide - high.astype(F32)).astype(BF)
    return dot(a, high) + dot(a, low)


def pick(mask):
    return jnp.where(mask, 1.0, 0.0).astype(BF)


def unit_back(raw, total, grad):
    inner = jnp.sum(raw * grad, axis=-1, keepdims=True)
    inv = lax.rsqrt(total)
    return grad * inv - raw * (inner * inv / total)


class Link:
    def __init__(self, made):
        self.made, self.started, self.arrived = made, False, False

    def start(self):
        self.started = True
        self.made.start()

    def wait_recv(self):
        self.arrived = True
        self.made.wait_recv()


class Sems:
    def __init__(self, send, recv):
        self.send, self.recv, self.used = send, recv, 0
        self.open = []

    def copy(self, src, dst, device):
        i = self.used
        self.used += 1
        made = Link(pltpu.make_async_remote_copy(
            src_ref=src, dst_ref=dst, send_sem=self.send.at[i], recv_sem=self.recv.at[i],
            device_id=device, device_id_type=MESH,
        ))
        self.open.append(made)
        return made

    def finish(self):
        for one in self.open:
            if one.started and not one.arrived:
                one.wait_recv()
        for one in self.open:
            if one.started:
                one.made.wait_send()


def n_sems(sizes):
    nx, ny, nz, nc = sizes
    y, z, x, c = ny - 1, nz - 1, nx - 1, nc - 1
    gather = 2 * y + 2 * y * (ny // 2 + 1)
    items = 2 * (y + z) * 2 + (y + z)
    groups = ny // 2 + 1
    reduce = 2 * (c + groups * x + y + z + y + groups * (x + c * nx))
    return gather + items + reduce


def kernel(sizes, q_hbm, qw_hbm, iw_hbm, t_hbm, r_ref, req_ref, inv_ref, fin, fresh_ref,
           q_ref, qw_ref, iw_ref, t_ref, local_sem, id_ref, buf, qt, tt, traw, qraw, qe, wacc, dacc, mt, ot, iraw, pos, pos_expo,
           id1, id2, id2s, rs1, rr1, rs2, rr2, fs1, fr1, fs2, fr2, bs1, br1, bs2, br2,
           term, sc, rc, sx, rx, sy, ry, mine_f32, zs, rz, send_sem, recv_sem):
    nx, ny, nz, nc = sizes
    ns = ny * nz
    slots = ns * CAP
    d, s = lax.axis_index("dp"), lax.axis_index("shard")
    x, core = lax.div(d, nc), lax.rem(d, nc)
    y, z = lax.div(s, nz), lax.rem(s, nz)
    at_y = lambda p: (d, p * nz + z)
    at_z = lambda p: (d, y * nz + p)
    at_x = lambda p: (p * nc + core, s)
    at_c = lambda p: (x * nc + p, s)
    sems = Sems(send_sem, recv_sem)
    local = [
        pltpu.make_async_copy(src, dst, local_sem.at[i])
        for i, (src, dst) in enumerate((
            (t_hbm, t_ref), (iw_hbm, iw_ref), (q_hbm, q_ref), (qw_hbm, qw_ref),
            (r_ref.at[pl.ds(0, r_ref.shape[0] // 2)], buf.at[0, 0, 0]),
            (r_ref.at[pl.ds(r_ref.shape[0] // 2, r_ref.shape[0] // 2)], buf.at[1, 0, 0]),
        ))
    ]
    for one in local:
        one.start()
    lane = lax.broadcasted_iota(jnp.int32, (CAP, slots), 1)
    spot = lax.broadcasted_iota(jnp.int32, (CAP, slots), 0)
    asks = jnp.maximum(req_ref[...], 0).astype(F32)
    id_ref[...] = dot(asks, jnp.where(lane == s * CAP + spot, 1.0, 0.0), 0, 0).astype(jnp.int32)

    barrier = pltpu.get_barrier_semaphore()
    total = 0
    for at, n, me in ((at_y, ny, y), (at_z, nz, z), (at_x, nx, x), (at_c, nc, core)):
        for k in range(1, n):
            pl.semaphore_signal(barrier, inc=1, device_id=at(lax.rem(me + k, n)), device_id_type=MESH)
            total += 1
    pl.semaphore_wait(barrier, total)

    def exchange(at, n, me, src, dst):
        made = []
        for k in range(1, n):
            p = lax.rem(me + k, n)
            made.append(sems.copy(src(p), dst(me), at(p)))
        for one in made:
            one.start()
        return made

    def arrive(made):
        for one in made:
            one.wait_recv()

    n = ny
    half = r_ref.shape[0] // 2
    far = n // 2
    pieces = [(0, 1)] + [(2 * k - 1, 2) for k in range(1, far)] + [(n - 1, 1)]
    rightward = {0, far} | set(range(1, n // 4))

    def slot(offset):
        return n - 1 if abs(offset) == far else 2 * offset - 1 if offset > 0 else -2 * offset

    first, second = {}, {}
    axes = (((at_y, y), (at_z, z)), ((at_z, z), (at_y, y)))
    for h in (0, 1):
        (at1, me1), (at2, me2) = axes[h]
        for left in (0, 1):
            turn = 1 if left else -1
            hop = n - 1 if left else 1
            to2 = at2(lax.rem(me2 + hop, n))
            for k in range(1, far + 1):
                if k < far or left == h:
                    src, hops = (r_ref.at[pl.ds(h * half, half)], k) if k < 3 else (buf.at[h, 0, slot(turn * 2)], k - 2)
                    to1 = at1(lax.rem(me1 + hops * hop, n))
                    first[h, left, k] = sems.copy(src, buf.at[h, 0, slot(turn * k)], to1)
                for p, (begin, size) in enumerate(pieces):
                    if k < far or (p in rightward) == (left == 0):
                        at = pl.ds(begin, size)
                        src, dst = buf.at[h, slot(turn * (k - 1)), at], buf.at[h, slot(turn * k), at]
                        if k == 1 and p == 0:
                            src, dst = r_ref.at[pl.ds(h * half, half)], buf.at[h, slot(turn), 0]
                        second[h, left, k, p] = sems.copy(src, dst, to2)

    streams = [(h, left) for h in (0, 1) for left in (0, 1)]

    def send_first(*distances):
        for k in distances:
            for h, left in streams:
                if (h, left, k) in first:
                    first[h, left, k].start()

    def have_first(*distances):
        for k in distances:
            for h, left in streams:
                if (h, left, k) in first:
                    first[h, left, k].wait_recv()

    def send_column(*which):
        for p in which:
            for h, left in streams:
                if (h, left, 1, p) in second:
                    second[h, left, 1, p].start()

    def ring(k, *which):
        for p in which:
            for h, left in streams:
                if (h, left, k, p) in second:
                    second[h, left, k, p].wait_recv()
                    if (h, left, k + 1, p) in second:
                        second[h, left, k + 1, p].start()

    attended = set()

    def attend(*which):
        parts = []
        for h in (0, 1):
            for offset in which:
                if abs(offset) > far or (h, slot(offset)) in attended:
                    continue
                attended.add((h, slot(offset)))
                rows = buf[h, slot(offset)]
                keys = rows.reshape(n * half, rows.shape[2])
                parts.append((keys, jnp.exp2(dot(qe[...], keys, 1, 1) * (SCALE * LOG2E))))
        if parts:
            wacc[...] += sum(dot(expo.astype(BF), keys) for keys, expo in parts)
            lanes = dacc.shape[1]
            dacc[...] += sum(expo[:, k : k + lanes] for _, expo in parts for k in range(0, expo.shape[1], lanes))

    def slot_of(i):
        zo, yo, c = i // (ny * CAP), (i // CAP) % ny, i % CAP
        return (yo * nz + zo) * CAP + c

    square = (slots, slots)
    send_first(1, 2)
    ids_y = exchange(at_y, ny, y, lambda p: id_ref.at[pl.ds(pl.multiple_of(p * nz, nz), nz)], lambda me: id1.at[me])
    send_column(0)
    id1[y] = id_ref[pl.ds(pl.multiple_of(y * nz, nz), nz), :]
    wacc[...] = jnp.zeros_like(wacc)
    dacc[...] = jnp.zeros_like(dacc)
    local[0].wait()
    local[1].wait()
    traw[...] = dot(t_ref[...], iw_ref[...]).astype(BF)
    have_first(1, 2)
    send_first(3, 4)
    send_column(1, 2)
    ring(1, 0)
    for one in local[2:]:
        one.wait()
    raw = dot(q_ref[...], qw_ref[...])
    qraw[...] = raw
    q_total = jnp.sum(raw * raw, axis=-1, keepdims=True) + EPS
    qe[...] = (raw * lax.rsqrt(q_total)).astype(BF)
    arrive(ids_y)
    id2s[...] = jnp.sum(id1[...], axis=0)
    id2[z] = id2s[...]
    ids_z = exchange(at_z, nz, z, lambda p: id2s, lambda me: id2.at[me])
    have_first(3, 4)
    send_column(3, 4)
    ring(1, 1)
    qt[...] = q_ref[...].T
    ring(1, 2)

    arrive(ids_z)
    mine = lax.broadcasted_iota(jnp.int32, (nz, slots), 0) == z
    asked = jnp.sum(jnp.where(mine, jnp.sum(id2[...], axis=0), 0), axis=0, keepdims=True)
    mt[...] = pick(lax.broadcasted_iota(jnp.int32, mt.shape, 0) == asked)
    rs1[...] = dot(mt[...], traw[...], 0, 0).astype(BF).reshape(rs1.shape)
    rr1[y] = rs1[y]
    rows_y = exchange(at_y, ny, y, lambda p: rs1.at[p], lambda me: rr1.at[me])
    ring(1, 3)
    attend(0)
    ring(1, 4)
    ring(2, 0, 1)
    attend(-1)
    ring(2, 2, 3)
    attend(1)
    ring(2, 4)
    arrive(rows_y)
    order = pick(lax.broadcasted_iota(jnp.int32, square, 1) == slot_of(lax.broadcasted_iota(jnp.int32, square, 0)))
    rs2[...] = dot(order, rr1[...].reshape(slots, -1)).astype(BF).reshape(rs2.shape)
    rr2[z] = rs2[z]
    rows_z = exchange(at_z, nz, z, lambda p: rs2.at[p], lambda me: rr2.at[me])
    ring(3, 0, 1)
    attend(-2)
    ring(3, 2, 3)
    attend(2)
    ring(3, 4)
    tt[...] = t_ref[...].T

    attend(-3, 3)
    ring(4, 0, 1)
    arrive(rows_z)
    item = rr2[...].reshape(slots, -1).astype(F32)
    iraw[...] = item
    i_total = jnp.sum(item * item, axis=-1, keepdims=True) + EPS
    embed = (item * lax.rsqrt(i_total)).astype(BF)
    slot_rows = slot_of(lax.broadcasted_iota(jnp.int32, ot.shape, 0))
    ot[...] = pick(slot_rows == inv_ref[...])
    pos[...] = dot(ot[...], embed, 0, 0)
    pos_expo[...] = jnp.exp(SCALE * jnp.sum(qe[...].astype(F32) * pos[...], axis=1, keepdims=True))
    head = jnp.broadcast_to(pos[0:1, :], fs1.shape)
    fs1[...] = jnp.where(lax.broadcasted_iota(jnp.int32, fs1.shape, 0) == y, head, 0.0).astype(BF)
    fr1[y] = fs1[...]
    fresh_y = exchange(at_y, ny, y, lambda p: fs1, lambda me: fr1.at[me])
    ring(4, 2, 3, 4)
    attend(-4)

    raw = qraw[...]
    q_total = jnp.sum(raw * raw, axis=-1, keepdims=True) + EPS
    embed = qe[...].astype(F32)
    positive = pos[...]
    denom = pos_expo[...] + jnp.sum(dacc[...], axis=1, keepdims=True)
    less = pos_expo[...] / denom - 1.0
    item_grad = split_dot(ot[...], (SCALE * less) * embed)
    item = iraw[...]
    i_total = jnp.sum(item * item, axis=-1, keepdims=True) + EPS
    bs1[...] = unit_back(item, i_total, item_grad).astype(BF).reshape(bs1.shape)
    br1[z] = bs1[z]
    back_z = exchange(at_z, nz, z, lambda p: bs1.at[p], lambda me: br1.at[me])
    query_grad = SCALE * (wacc[...] / denom + less * positive)
    query_back = unit_back(raw, q_total, query_grad).astype(BF)

    part = term.shape[1] // nc

    def core_send(a):
        if nc == 1:
            return []
        other = pl.multiple_of((1 - core) * part, part)
        sc[a] = term[a, pl.ds(other, part), :].astype(BF)
        return exchange(at_c, nc, core, lambda p: sc.at[a], lambda me: rc.at[a])

    def core_sum(a):
        own = term[a, pl.ds(pl.multiple_of(core * part, part), part), :]
        return own + rc[a].astype(F32) if nc > 1 else own

    px, py = part // nx, part // nx // ny
    offsets = [0] + [turn * k for k in range(1, far) for turn in (1, -1)] + [far]
    groups = [(p,) + piece for p, piece in enumerate(pieces)]
    across = {}
    along = {}

    def x_send(a):
        term[a, pl.ds(0, part), :] = core_sum(a)
        for j, offset in enumerate(offsets):
            yy = lax.rem(y + offset + ny, ny)
            for xx in range(nx):
                rows = pl.ds(pl.multiple_of(xx * px + yy * py, py), py)
                sx[a, xx, j] = term[a, rows, :].astype(BF)
        for p, begin, size in groups[::-1]:
            for k in range(1, nx):
                to = lax.rem(x + k, nx)
                at = pl.ds(begin, size)
                across[a, p, k] = sems.copy(sx.at[a, to, at], rx.at[a, x, at], at_x(to))
                across[a, p, k].start()

    def y_send(a):
        for p, begin, size in groups[::-1]:
            for k in range(1, nx):
                across[a, p, k].wait_recv()
            for j in range(begin, begin + size):
                yy = lax.rem(y + offsets[j] + ny, ny)
                value = term[a, pl.ds(pl.multiple_of(x * px + yy * py, py), py), :]
                for k in range(1, nx):
                    value = value + rx[a, lax.rem(x + k, nx), j].astype(F32)
                if j == 0:
                    mine_f32[a] = value
                else:
                    sy[a, j] = value.astype(BF)
                    back = slot(-offsets[j]) if j < ny - 1 else ny - 1
                    along[a, j] = sems.copy(sy.at[a, j], ry.at[a, back], at_y(yy))
                    along[a, j].start()

    def z_send(a):
        value = mine_f32[a]
        for j in range(1, ny):
            along[a, j].wait_recv()
        for j in range(1, ny):
            value = value + ry[a, j].astype(F32)
        zs[a] = value.astype(BF)
        rz[a, z] = zs[a]
        return exchange(at_z, nz, z, lambda p: zs.at[a], lambda me: rz.at[a, me])

    out_y, out_x, to_core = {}, {}, {0: [], 1: []}

    def hand_over(a, xx, begin, size):
        if nc > 1:
            ref = fin.at[a, core, xx, pl.ds(begin, size)]
            to_core[a].append(sems.copy(ref, ref, at_c(1 - core)))
            to_core[a][-1].start()

    def out_send(a, p, begin, size):
        ref = fin.at[a, core, x, pl.ds(begin, size)]
        for k in range(1, nx):
            out_x[a, p, k] = sems.copy(ref, ref, at_x(lax.rem(x + k, nx)))
            out_x[a, p, k].start()
        hand_over(a, x, begin, size)

    def gather_send(a, arrived):
        arrive(arrived)
        fin[a, core, x, 0] = jnp.sum(rz[a].astype(F32), axis=0).astype(BF)
        for k in range(1, ny):
            offset = ny - k if ny - k <= far else -k
            out_y[a, k] = sems.copy(fin.at[a, core, x, 0], fin.at[a, core, x, slot(offset)], at_y(lax.rem(y + k, ny)))
            out_y[a, k].start()
        out_send(a, *groups[0])

    def gather_x(a):
        for p, begin, size in groups[1:]:
            for k in sorted({p, ny - p}):
                out_y[a, k].wait_recv()
            out_send(a, p, begin, size)

    def gather_core(a):
        for p, begin, size in groups:
            for k in range(1, nx):
                out_x[a, p, k].wait_recv()
                hand_over(a, lax.rem(x + nx - k, nx), begin, size)

    arrive(fresh_y)
    fs2[...] = jnp.sum(fr1[...].astype(F32), axis=0).astype(BF)
    fr2[z] = fs2[...]
    fresh_z = exchange(at_z, nz, z, lambda p: fs2, lambda me: fr2.at[me])

    term[0] = dot(qt[...], query_back)
    c_q = core_send(0)
    arrive(c_q)
    x_send(0)
    arrive(back_z)
    order = pick(lax.broadcasted_iota(jnp.int32, square, 0) == slot_of(lax.broadcasted_iota(jnp.int32, square, 1)))
    bs2[...] = dot(order, br1[...].reshape(slots, -1)).astype(BF).reshape(bs2.shape)
    br2[y] = bs2[y]
    back_y = exchange(at_y, ny, y, lambda p: bs2.at[p], lambda me: br2.at[me])
    y_send(0)
    arrive(back_y)
    owned = dot(mt[...], br2[...].reshape(slots, -1))
    term[1] = split_dot(tt[...], owned)
    c_i = core_send(1)
    z_q = z_send(0)
    arrive(c_i)
    x_send(1)
    gather_send(0, z_q)
    y_send(1)
    gather_x(0)
    z_i = z_send(1)
    gather_core(0)
    arrive(fresh_z)
    fshape = (ns, nz * fs2.shape[0])
    want = lax.broadcasted_iota(jnp.int32, fshape, 0)
    place = (want % nz) * fs2.shape[0] + want // nz
    fresh_ref[...] = dot(pick(lax.broadcasted_iota(jnp.int32, fshape, 1) == place),
                         fr2[...].reshape(fshape[1], -1)).astype(BF)
    arrive(to_core[0])
    gather_send(1, z_i)
    gather_x(1)
    gather_core(1)
    arrive(to_core[1])
    sems.finish()


def clip(nz, sums_ref, fresh_ref, queue_ref, owner_ref, outq, outi, outn, sq, si, sn, sem):
    s = lax.axis_index("shard")
    ny = sums_ref.shape[3]
    y = lax.div(s, nz)
    ns = fresh_ref.shape[0]
    mine = owner_ref[0] == s
    sn[pl.ds(0, ns), :] = jnp.where(mine, fresh_ref[...], queue_ref[pl.ds(0, ns), :])
    sn[pl.ds(ns, sn.shape[0] - ns), :] = queue_ref[pl.ds(ns, sn.shape[0] - ns), :]
    made = [pltpu.make_async_copy(src, dst, sem.at[i]) for i, (src, dst) in enumerate(((sn, outn), (sq, outq), (si, outi)))]
    made[0].start()
    sums = sums_ref[...].astype(F32)
    squares = jnp.sum(jnp.sum(sums * sums, axis=(0, 1, 2, 3)), keepdims=True)
    count = math.prod(sums_ref.shape)
    factor = jnp.minimum(1.0, math.sqrt(count) / jnp.sqrt(squares + EPS))
    for a, out in enumerate((sq, si)):
        for row in range(ny):
            ahead = lax.rem(row - y + ny, ny)
            at = jnp.where(ahead == 0, 0, jnp.where(ahead < ny // 2, 2 * ahead - 1, 2 * (ny - ahead)))
            at = jnp.where(ahead == ny // 2, ny - 1, at)
            out[:, :, row] = (sums_ref[a, :, :, at].astype(F32) * factor).astype(BF)
        made[1 + a].start()
    for one in made:
        one.wait()


def per_device(sizes, queries, query_weight, item_weight, table, queue, requests, inverse, write_owner):
    nx, ny, nz, nc = sizes
    ns = ny * nz
    slots = ns * CAP
    width, embed = query_weight.shape
    n_q, n_t = queries.shape[0], table.shape[0]
    n_r = queue.shape[0] // 2
    s = lax.axis_index("shard")
    part = width // nc
    px, py = part // nx, part // nx // ny
    vm = lambda shape, dtype: pltpu.VMEM(shape, dtype)
    zrows, yrows = ny * CAP, nz * CAP
    scratch = [
        vm(queries.shape, BF),
        vm(query_weight.shape, BF),
        vm(item_weight.shape, BF),
        vm(table.shape, BF),
        pltpu.SemaphoreType.DMA((6,)),
        vm((ns, slots), jnp.int32),
        vm((2, nz, ny, n_r, embed), BF),
        vm((width, n_q), BF),
        vm((width, n_t), BF),
        vm((n_t, embed), BF),
        vm((n_q, embed), F32),
        vm((n_q, embed), BF),
        vm((n_q, embed), F32),
        vm((n_q, 128), F32),
        vm((n_t, slots), BF),
        vm((slots, n_q), BF),
        vm((slots, embed), F32),
        vm((n_q, embed), F32),
        vm((n_q, 1), F32),
        vm((ny, nz, slots), jnp.int32),
        vm((nz, nz, slots), jnp.int32),
        vm((nz, slots), jnp.int32),
        vm((ny, yrows, embed), BF),
        vm((ny, yrows, embed), BF),
        vm((nz, zrows, embed), BF),
        vm((nz, zrows, embed), BF),
        vm((16, embed), BF),
        vm((ny, 16, embed), BF),
        vm((16, embed), BF),
        vm((nz, 16, embed), BF),
        vm((nz, zrows, embed), BF),
        vm((nz, zrows, embed), BF),
        vm((ny, yrows, embed), BF),
        vm((ny, yrows, embed), BF),
        vm((2, width, embed), F32),
        vm((2, part, embed), BF),
        vm((2, part, embed), BF),
        vm((2, nx, ny, py, embed), BF),
        vm((2, nx, ny, py, embed), BF),
        vm((2, ny, py, embed), BF),
        vm((2, ny, py, embed), BF),
        vm((2, py, embed), F32),
        vm((2, py, embed), BF),
        vm((2, nz, py, embed), BF),
        pltpu.SemaphoreType.DMA((n_sems(sizes),)),
        pltpu.SemaphoreType.DMA((n_sems(sizes),)),
    ]
    full = pl.BlockSpec(memory_space=pltpu.VMEM)
    far = pl.BlockSpec(memory_space=pl.ANY)
    sums, fresh = pl.pallas_call(
        functools.partial(kernel, sizes),
        out_shape=[
            jax.ShapeDtypeStruct((2, nc, nx, ny, py, embed), BF),
            jax.ShapeDtypeStruct((ns, embed), BF),
        ],
        in_specs=[far] * 5 + [full] * 2,
        out_specs=[full] * 2,
        scratch_shapes=scratch,
        compiler_params=pltpu.CompilerParams(
            collective_id=0, has_side_effects=True, vmem_limit_bytes=56 * 2**20
        ),
        name="step",
    )(queries, query_weight, item_weight, table, queue, requests.T, inverse.reshape(1, n_q))
    laid = (nc, nx, ny, py, embed)
    out_q, out_i, new_queue = pl.pallas_call(
        functools.partial(clip, nz),
        out_shape=[
            jax.ShapeDtypeStruct(laid, BF),
            jax.ShapeDtypeStruct(laid, BF),
            jax.ShapeDtypeStruct(queue.shape, BF),
        ],
        in_specs=[full] * 3 + [pl.BlockSpec(memory_space=pltpu.SMEM)],
        out_specs=[far] * 3,
        scratch_shapes=[
            vm(laid, BF),
            vm(laid, BF),
            vm(queue.shape, BF),
            pltpu.SemaphoreType.DMA((3,)),
        ],
        name="clip",
    )(sums, fresh, queue, write_owner)
    return out_q.reshape(width, embed), out_i.reshape(width, embed), new_queue


def solution(mesh, sizes=(4, 8, 8, 2)):
    placed = (
        P(("dp", "shard"), None),
        P(),
        P(),
        P("shard", None),
        P(("dp", "shard"), None),
        P(("dp", "shard"), None),
        P(("dp", "shard")),
        P(),
    )
    return jax.shard_map(
        functools.partial(per_device, sizes),
        mesh=mesh,
        in_specs=placed,
        out_specs=(P(), P(), P(("dp", "shard"), None)),
        check_vma=False,
    )
```

```python
import functools
import math

import jax
import jax.numpy as jnp
from jax import lax
from jax.experimental import pallas as pl
from jax.experimental.pallas import tpu as pltpu
from jax.sharding import PartitionSpec as P

SCALE = 50.0
EPS = 1e-06
CAP = 4
BF = jnp.bfloat16
F32 = jnp.float32
LOG2E = math.log2(math.e)
MESH = pl.DeviceIdType.MESH


def dot(a, b, lhs=1, rhs=0):
    return lax.dot_general(a, b, (((lhs,), (rhs,)), ((), ())), preferred_element_type=F32)


def split_dot(a, wide):
    high = wide.astype(BF)
    low = (wide - high.astype(F32)).astype(BF)
    return dot(a, high) + dot(a, low)


def pick(mask):
    return jnp.where(mask, 1.0, 0.0).astype(BF)


def unit_back(raw, total, grad):
    inner = jnp.sum(raw * grad, axis=-1, keepdims=True)
    inv = lax.rsqrt(total)
    return grad * inv - raw * (inner * inv / total)


class Link:
    def __init__(self, made):
        self.made, self.started, self.arrived, self.sent = made, False, False, False

    def start(self):
        self.started = True
        self.made.start()

    def wait_recv(self):
        self.arrived = True
        self.made.wait_recv()


class Sems:
    def __init__(self, send, recv):
        self.send, self.recv, self.used = send, recv, 0
        self.open = []

    def copy(self, src, dst, device):
        i = self.used
        self.used += 1
        made = Link(pltpu.make_async_remote_copy(
            src_ref=src, dst_ref=dst, send_sem=self.send.at[i], recv_sem=self.recv.at[i],
            device_id=device, device_id_type=MESH,
        ))
        self.open.append(made)
        return made

    def drain(self):
        for one in self.open:
            if one.started and one.arrived and not one.sent:
                one.sent = True
                one.made.wait_send()

    def finish(self):
        for one in self.open:
            if one.started and not one.arrived:
                one.wait_recv()
        for one in self.open:
            if one.started and not one.sent:
                one.made.wait_send()


def n_sems(sizes):
    nx, ny, nz, nc = sizes
    y, z, x, c = ny - 1, nz - 1, nx - 1, nc - 1
    gather = 2 * y + 2 * y * (ny // 2 + 1)
    items = 2 * (y + z) * 2 + (y + z)
    groups = ny // 2 + 1
    reduce = 2 * (c + groups * x + y + z + y + groups * (x + c * nx))
    return gather + items + reduce


def kernel(sizes, q_hbm, qw_hbm, iw_hbm, t_hbm, r_ref, req_ref, inv_ref, fin, fresh_ref,
           q_ref, qw_ref, iw_ref, t_ref, local_sem, id_ref, buf, qt, tt, traw, qraw, qe, wacc, dacc, mt, ot, iraw, pos, pos_expo,
           id1, id2, id2s, rs1, rr1, rs2, rr2, fs1, fr1, fs2, fr2, bs1, br1, bs2, br2,
           term, sc, rc, sx, rx, sy, ry, mine_f32, zs, rz, send_sem, recv_sem):
    nx, ny, nz, nc = sizes
    ns = ny * nz
    slots = ns * CAP
    d, s = lax.axis_index("dp"), lax.axis_index("shard")
    x, core = lax.div(d, nc), lax.rem(d, nc)
    y, z = lax.div(s, nz), lax.rem(s, nz)
    at_y = lambda p: (d, p * nz + z)
    at_z = lambda p: (d, y * nz + p)
    at_x = lambda p: (p * nc + core, s)
    at_c = lambda p: (x * nc + p, s)
    sems = Sems(send_sem, recv_sem)
    local = [
        pltpu.make_async_copy(src, dst, local_sem.at[i])
        for i, (src, dst) in enumerate((
            (t_hbm, t_ref), (iw_hbm, iw_ref), (q_hbm, q_ref), (qw_hbm, qw_ref),
            (r_ref.at[pl.ds(0, r_ref.shape[0] // 2)], buf.at[0, 0, 0]),
            (r_ref.at[pl.ds(r_ref.shape[0] // 2, r_ref.shape[0] // 2)], buf.at[1, 0, 0]),
        ))
    ]
    for one in local:
        one.start()
    lane = lax.broadcasted_iota(jnp.int32, (CAP, slots), 1)
    spot = lax.broadcasted_iota(jnp.int32, (CAP, slots), 0)
    asks = jnp.maximum(req_ref[...], 0).astype(F32)
    id_ref[...] = dot(asks, jnp.where(lane == s * CAP + spot, 1.0, 0.0), 0, 0).astype(jnp.int32)

    barrier = pltpu.get_barrier_semaphore()
    total = 0
    for at, n, me in ((at_y, ny, y), (at_z, nz, z), (at_x, nx, x), (at_c, nc, core)):
        for k in range(1, n):
            pl.semaphore_signal(barrier, inc=1, device_id=at(lax.rem(me + k, n)), device_id_type=MESH)
            total += 1
    pl.semaphore_wait(barrier, total)

    def exchange(at, n, me, src, dst):
        made = []
        for k in range(1, n):
            p = lax.rem(me + k, n)
            made.append(sems.copy(src(p), dst(me), at(p)))
        for one in made:
            one.start()
        return made

    def arrive(made):
        for one in made:
            one.wait_recv()

    n = ny
    half = r_ref.shape[0] // 2
    far = n // 2
    pieces = [(0, 1)] + [(2 * k - 1, 2) for k in range(1, far)] + [(n - 1, 1)]
    rightward = {0, far} | set(range(1, n // 4))

    def slot(offset):
        return n - 1 if abs(offset) == far else 2 * offset - 1 if offset > 0 else -2 * offset

    first, second = {}, {}
    axes = (((at_y, y), (at_z, z)), ((at_z, z), (at_y, y)))
    for h in (0, 1):
        (at1, me1), (at2, me2) = axes[h]
        for left in (0, 1):
            turn = 1 if left else -1
            hop = n - 1 if left else 1
            to2 = at2(lax.rem(me2 + hop, n))
            for k in range(1, far + 1):
                if k < far or left == h:
                    src, hops = (r_ref.at[pl.ds(h * half, half)], k) if k < 3 else (buf.at[h, 0, slot(turn * 2)], k - 2)
                    to1 = at1(lax.rem(me1 + hops * hop, n))
                    first[h, left, k] = sems.copy(src, buf.at[h, 0, slot(turn * k)], to1)
                for p, (begin, size) in enumerate(pieces):
                    if k < far or (p in rightward) == (left == 0):
                        at = pl.ds(begin, size)
                        src, dst = buf.at[h, slot(turn * (k - 1)), at], buf.at[h, slot(turn * k), at]
                        if k == 1 and p == 0:
                            src, dst = r_ref.at[pl.ds(h * half, half)], buf.at[h, slot(turn), 0]
                        second[h, left, k, p] = sems.copy(src, dst, to2)

    streams = [(h, left) for h in (0, 1) for left in (0, 1)]

    def send_first(*distances):
        for k in distances:
            for h, left in streams:
                if (h, left, k) in first:
                    first[h, left, k].start()

    def have_first(*distances):
        for k in distances:
            for h, left in streams:
                if (h, left, k) in first:
                    first[h, left, k].wait_recv()

    def send_column(*which):
        for p in which:
            for h, left in streams:
                if (h, left, 1, p) in second:
                    second[h, left, 1, p].start()

    def ring(k, *which):
        for p in which:
            for h, left in streams:
                if (h, left, k, p) in second:
                    second[h, left, k, p].wait_recv()
                    if (h, left, k + 1, p) in second:
                        second[h, left, k + 1, p].start()

    attended = set()

    def attend(*which):
        parts = []
        for h in (0, 1):
            for offset in which:
                if abs(offset) > far or (h, slot(offset)) in attended:
                    continue
                attended.add((h, slot(offset)))
                rows = buf[h, slot(offset)]
                keys = rows.reshape(n * half, rows.shape[2])
                parts.append((keys, jnp.exp2(dot(qe[...], keys, 1, 1) * (SCALE * LOG2E))))
        if parts:
            wacc[...] += sum(dot(expo.astype(BF), keys) for keys, expo in parts)
            lanes = dacc.shape[1]
            dacc[...] += sum(expo[:, k : k + lanes] for _, expo in parts for k in range(0, expo.shape[1], lanes))

    def slot_of(i):
        zo, yo, c = i // (ny * CAP), (i // CAP) % ny, i % CAP
        return (yo * nz + zo) * CAP + c

    square = (slots, slots)
    send_first(1, 2)
    ids_y = exchange(at_y, ny, y, lambda p: id_ref.at[pl.ds(pl.multiple_of(p * nz, nz), nz)], lambda me: id1.at[me])
    send_column(0)
    id1[y] = id_ref[pl.ds(pl.multiple_of(y * nz, nz), nz), :]
    wacc[...] = jnp.zeros_like(wacc)
    dacc[...] = jnp.zeros_like(dacc)
    local[0].wait()
    local[1].wait()
    traw[...] = dot(t_ref[...], iw_ref[...]).astype(BF)
    have_first(1, 2)
    send_first(3, 4)
    send_column(1, 2)
    ring(1, 0)
    for one in local[2:]:
        one.wait()
    raw = dot(q_ref[...], qw_ref[...])
    qraw[...] = raw
    q_total = jnp.sum(raw * raw, axis=-1, keepdims=True) + EPS
    qe[...] = (raw * lax.rsqrt(q_total)).astype(BF)
    arrive(ids_y)
    id2s[...] = jnp.sum(id1[...], axis=0)
    id2[z] = id2s[...]
    ids_z = exchange(at_z, nz, z, lambda p: id2s, lambda me: id2.at[me])
    have_first(3, 4)
    send_column(3, 4)
    ring(1, 1)
    ring(1, 2)

    arrive(ids_z)
    mine = lax.broadcasted_iota(jnp.int32, (nz, slots), 0) == z
    asked = jnp.sum(jnp.where(mine, jnp.sum(id2[...], axis=0), 0), axis=0, keepdims=True)
    mt[...] = pick(lax.broadcasted_iota(jnp.int32, mt.shape, 0) == asked)
    rs1[...] = dot(mt[...], traw[...], 0, 0).astype(BF).reshape(rs1.shape)
    rr1[y] = rs1[y]
    rows_y = exchange(at_y, ny, y, lambda p: rs1.at[p], lambda me: rr1.at[me])
    ring(1, 3)
    attend(0)
    ring(1, 4)
    ring(2, 0, 1)
    attend(-1)
    ring(2, 2, 3)
    attend(1)
    ring(2, 4)
    arrive(rows_y)
    order = pick(lax.broadcasted_iota(jnp.int32, square, 1) == slot_of(lax.broadcasted_iota(jnp.int32, square, 0)))
    rs2[...] = dot(order, rr1[...].reshape(slots, -1)).astype(BF).reshape(rs2.shape)
    rr2[z] = rs2[z]
    rows_z = exchange(at_z, nz, z, lambda p: rs2.at[p], lambda me: rr2.at[me])
    ring(3, 0, 1)
    attend(-2)
    ring(3, 2, 3)
    attend(2)
    ring(3, 4)

    attend(-3, 3)
    ring(4, 0, 1)
    arrive(rows_z)
    item = rr2[...].reshape(slots, -1).astype(F32)
    iraw[...] = item
    i_total = jnp.sum(item * item, axis=-1, keepdims=True) + EPS
    embed = (item * lax.rsqrt(i_total)).astype(BF)
    slot_rows = slot_of(lax.broadcasted_iota(jnp.int32, ot.shape, 0))
    ot[...] = pick(slot_rows == inv_ref[...])
    pos[...] = dot(ot[...], embed, 0, 0)
    pos_expo[...] = jnp.exp(SCALE * jnp.sum(qe[...].astype(F32) * pos[...], axis=1, keepdims=True))
    ring(4, 2, 3, 4)
    attend(-4)

    raw = qraw[...]
    q_total = jnp.sum(raw * raw, axis=-1, keepdims=True) + EPS
    embed = qe[...].astype(F32)
    positive = pos[...]
    denom = pos_expo[...] + jnp.sum(dacc[...], axis=1, keepdims=True)
    less = pos_expo[...] / denom - 1.0
    item_grad = split_dot(ot[...], (SCALE * less) * embed)
    item = iraw[...]
    i_total = jnp.sum(item * item, axis=-1, keepdims=True) + EPS
    bs1[...] = unit_back(item, i_total, item_grad).astype(BF).reshape(bs1.shape)
    br1[z] = bs1[z]
    back_z = exchange(at_z, nz, z, lambda p: bs1.at[p], lambda me: br1.at[me])
    head = jnp.broadcast_to(pos[0:1, :], fs1.shape)
    fs1[...] = jnp.where(lax.broadcasted_iota(jnp.int32, fs1.shape, 0) == y, head, 0.0).astype(BF)
    fr1[y] = fs1[...]
    fresh_y = exchange(at_y, ny, y, lambda p: fs1, lambda me: fr1.at[me])
    qt[...] = q_ref[...].T
    query_grad = SCALE * (wacc[...] / denom + less * positive)
    query_back = unit_back(raw, q_total, query_grad).astype(BF)

    part = term.shape[1] // nc

    def core_send(a):
        if nc == 1:
            return []
        other = pl.multiple_of((1 - core) * part, part)
        sc[a] = term[a, pl.ds(other, part), :].astype(BF)
        return exchange(at_c, nc, core, lambda p: sc.at[a], lambda me: rc.at[a])

    def core_sum(a):
        own = term[a, pl.ds(pl.multiple_of(core * part, part), part), :]
        return own + rc[a].astype(F32) if nc > 1 else own

    px, py = part // nx, part // nx // ny
    offsets = [0] + [turn * k for k in range(1, far) for turn in (1, -1)] + [far]
    groups = [(p,) + piece for p, piece in enumerate(pieces)]
    across = {}
    along = {}

    def x_send(a):
        term[a, pl.ds(0, part), :] = core_sum(a)
        for j, offset in enumerate(offsets):
            yy = lax.rem(y + offset + ny, ny)
            for xx in range(nx):
                rows = pl.ds(pl.multiple_of(xx * px + yy * py, py), py)
                sx[a, xx, j] = term[a, rows, :].astype(BF)
        for p, begin, size in groups[::-1]:
            for k in range(1, nx):
                to = lax.rem(x + k, nx)
                at = pl.ds(begin, size)
                across[a, p, k] = sems.copy(sx.at[a, to, at], rx.at[a, x, at], at_x(to))
                across[a, p, k].start()

    def y_send(a):
        for p, begin, size in groups[::-1]:
            for k in range(1, nx):
                across[a, p, k].wait_recv()
            for j in range(begin, begin + size):
                yy = lax.rem(y + offsets[j] + ny, ny)
                value = term[a, pl.ds(pl.multiple_of(x * px + yy * py, py), py), :]
                for k in range(1, nx):
                    value = value + rx[a, lax.rem(x + k, nx), j].astype(F32)
                if j == 0:
                    mine_f32[a] = value
                else:
                    sy[a, j] = value.astype(BF)
                    back = slot(-offsets[j]) if j < ny - 1 else ny - 1
                    along[a, j] = sems.copy(sy.at[a, j], ry.at[a, back], at_y(yy))
                    along[a, j].start()

    def z_send(a):
        value = mine_f32[a]
        for j in range(1, ny):
            along[a, j].wait_recv()
        for j in range(1, ny):
            value = value + ry[a, j].astype(F32)
        zs[a] = value.astype(BF)
        rz[a, z] = zs[a]
        return exchange(at_z, nz, z, lambda p: zs.at[a], lambda me: rz.at[a, me])

    out_y, out_x, to_core = {}, {}, {0: [], 1: []}

    def hand_over(a, xx, begin, size):
        if nc > 1:
            ref = fin.at[a, core, xx, pl.ds(begin, size)]
            to_core[a].append(sems.copy(ref, ref, at_c(1 - core)))
            to_core[a][-1].start()

    def out_send(a, p, begin, size):
        ref = fin.at[a, core, x, pl.ds(begin, size)]
        for k in range(1, nx):
            out_x[a, p, k] = sems.copy(ref, ref, at_x(lax.rem(x + k, nx)))
            out_x[a, p, k].start()
        hand_over(a, x, begin, size)

    def gather_send(a, arrived):
        arrive(arrived)
        fin[a, core, x, 0] = jnp.sum(rz[a].astype(F32), axis=0).astype(BF)
        for k in range(1, ny):
            offset = ny - k if ny - k <= far else -k
            out_y[a, k] = sems.copy(fin.at[a, core, x, 0], fin.at[a, core, x, slot(offset)], at_y(lax.rem(y + k, ny)))
            out_y[a, k].start()
        out_send(a, *groups[0])

    def gather_x(a):
        for p, begin, size in groups[1:]:
            for k in sorted({p, ny - p}):
                out_y[a, k].wait_recv()
            out_send(a, p, begin, size)

    def gather_core(a):
        for p, begin, size in groups:
            for k in range(1, nx):
                out_x[a, p, k].wait_recv()
                hand_over(a, lax.rem(x + nx - k, nx), begin, size)

    term[0] = dot(qt[...], query_back)
    c_q = core_send(0)
    arrive(c_q)
    x_send(0)
    arrive(back_z)
    order = pick(lax.broadcasted_iota(jnp.int32, square, 0) == slot_of(lax.broadcasted_iota(jnp.int32, square, 1)))
    bs2[...] = dot(order, br1[...].reshape(slots, -1)).astype(BF).reshape(bs2.shape)
    br2[y] = bs2[y]
    back_y = exchange(at_y, ny, y, lambda p: bs2.at[p], lambda me: br2.at[me])
    y_send(0)
    tt[...] = t_ref[...].T
    arrive(fresh_y)
    fs2[...] = jnp.sum(fr1[...].astype(F32), axis=0).astype(BF)
    fr2[z] = fs2[...]
    fresh_z = exchange(at_z, nz, z, lambda p: fs2, lambda me: fr2.at[me])
    sems.drain()
    arrive(back_y)
    owned = dot(mt[...], br2[...].reshape(slots, -1))
    term[1] = split_dot(tt[...], owned)
    c_i = core_send(1)
    z_q = z_send(0)
    arrive(c_i)
    x_send(1)
    gather_send(0, z_q)
    y_send(1)
    gather_x(0)
    z_i = z_send(1)
    gather_core(0)
    sems.drain()
    arrive(fresh_z)
    fshape = (ns, nz * fs2.shape[0])
    want = lax.broadcasted_iota(jnp.int32, fshape, 0)
    place = (want % nz) * fs2.shape[0] + want // nz
    fresh_ref[...] = dot(pick(lax.broadcasted_iota(jnp.int32, fshape, 1) == place),
                         fr2[...].reshape(fshape[1], -1)).astype(BF)
    arrive(to_core[0])
    gather_send(1, z_i)
    gather_x(1)
    gather_core(1)
    sems.drain()
    arrive(to_core[1])
    sems.finish()


def clip(nz, sums_ref, fresh_ref, queue_ref, owner_ref, outq, outi, outn, sq, si, sn, sem):
    s = lax.axis_index("shard")
    ny = sums_ref.shape[3]
    y = lax.div(s, nz)
    ns = fresh_ref.shape[0]
    mine = owner_ref[0] == s
    sn[pl.ds(0, ns), :] = jnp.where(mine, fresh_ref[...], queue_ref[pl.ds(0, ns), :])
    sn[pl.ds(ns, sn.shape[0] - ns), :] = queue_ref[pl.ds(ns, sn.shape[0] - ns), :]
    made = [pltpu.make_async_copy(src, dst, sem.at[i]) for i, (src, dst) in enumerate(((sn, outn), (sq, outq), (si, outi)))]
    made[0].start()
    sums = sums_ref[...].astype(F32)
    squares = jnp.sum(jnp.sum(sums * sums, axis=(0, 1, 2, 3)), keepdims=True)
    count = math.prod(sums_ref.shape)
    factor = jnp.minimum(1.0, math.sqrt(count) / jnp.sqrt(squares + EPS))
    for a, out in enumerate((sq, si)):
        for row in range(ny):
            ahead = lax.rem(row - y + ny, ny)
            at = jnp.where(ahead == 0, 0, jnp.where(ahead < ny // 2, 2 * ahead - 1, 2 * (ny - ahead)))
            at = jnp.where(ahead == ny // 2, ny - 1, at)
            out[:, :, row] = (sums_ref[a, :, :, at].astype(F32) * factor).astype(BF)
        made[1 + a].start()
    for one in made:
        one.wait()


def per_device(sizes, queries, query_weight, item_weight, table, queue, requests, inverse, write_owner):
    nx, ny, nz, nc = sizes
    ns = ny * nz
    slots = ns * CAP
    width, embed = query_weight.shape
    n_q, n_t = queries.shape[0], table.shape[0]
    n_r = queue.shape[0] // 2
    s = lax.axis_index("shard")
    part = width // nc
    px, py = part // nx, part // nx // ny
    vm = lambda shape, dtype: pltpu.VMEM(shape, dtype)
    zrows, yrows = ny * CAP, nz * CAP
    scratch = [
        vm(queries.shape, BF),
        vm(query_weight.shape, BF),
        vm(item_weight.shape, BF),
        vm(table.shape, BF),
        pltpu.SemaphoreType.DMA((6,)),
        vm((ns, slots), jnp.int32),
        vm((2, nz, ny, n_r, embed), BF),
        vm((width, n_q), BF),
        vm((width, n_t), BF),
        vm((n_t, embed), BF),
        vm((n_q, embed), F32),
        vm((n_q, embed), BF),
        vm((n_q, embed), F32),
        vm((n_q, 128), F32),
        vm((n_t, slots), BF),
        vm((slots, n_q), BF),
        vm((slots, embed), F32),
        vm((n_q, embed), F32),
        vm((n_q, 1), F32),
        vm((ny, nz, slots), jnp.int32),
        vm((nz, nz, slots), jnp.int32),
        vm((nz, slots), jnp.int32),
        vm((ny, yrows, embed), BF),
        vm((ny, yrows, embed), BF),
        vm((nz, zrows, embed), BF),
        vm((nz, zrows, embed), BF),
        vm((16, embed), BF),
        vm((ny, 16, embed), BF),
        vm((16, embed), BF),
        vm((nz, 16, embed), BF),
        vm((nz, zrows, embed), BF),
        vm((nz, zrows, embed), BF),
        vm((ny, yrows, embed), BF),
        vm((ny, yrows, embed), BF),
        vm((2, width, embed), F32),
        vm((2, part, embed), BF),
        vm((2, part, embed), BF),
        vm((2, nx, ny, py, embed), BF),
        vm((2, nx, ny, py, embed), BF),
        vm((2, ny, py, embed), BF),
        vm((2, ny, py, embed), BF),
        vm((2, py, embed), F32),
        vm((2, py, embed), BF),
        vm((2, nz, py, embed), BF),
        pltpu.SemaphoreType.DMA((n_sems(sizes),)),
        pltpu.SemaphoreType.DMA((n_sems(sizes),)),
    ]
    full = pl.BlockSpec(memory_space=pltpu.VMEM)
    far = pl.BlockSpec(memory_space=pl.ANY)
    sums, fresh = pl.pallas_call(
        functools.partial(kernel, sizes),
        out_shape=[
            jax.ShapeDtypeStruct((2, nc, nx, ny, py, embed), BF),
            jax.ShapeDtypeStruct((ns, embed), BF),
        ],
        in_specs=[far] * 5 + [full] * 2,
        out_specs=[full] * 2,
        scratch_shapes=scratch,
        compiler_params=pltpu.CompilerParams(
            collective_id=0, has_side_effects=True, vmem_limit_bytes=56 * 2**20
        ),
        name="step",
    )(queries, query_weight, item_weight, table, queue, requests.T, inverse.reshape(1, n_q))
    laid = (nc, nx, ny, py, embed)
    out_q, out_i, new_queue = pl.pallas_call(
        functools.partial(clip, nz),
        out_shape=[
            jax.ShapeDtypeStruct(laid, BF),
            jax.ShapeDtypeStruct(laid, BF),
            jax.ShapeDtypeStruct(queue.shape, BF),
        ],
        in_specs=[full] * 3 + [pl.BlockSpec(memory_space=pltpu.SMEM)],
        out_specs=[far] * 3,
        scratch_shapes=[
            vm(laid, BF),
            vm(laid, BF),
            vm(queue.shape, BF),
            pltpu.SemaphoreType.DMA((3,)),
        ],
        name="clip",
    )(sums, fresh, queue, write_owner)
    return out_q.reshape(width, embed), out_i.reshape(width, embed), new_queue


def solution(mesh, sizes=(4, 8, 8, 2)):
    placed = (
        P(("dp", "shard"), None),
        P(),
        P(),
        P("shard", None),
        P(("dp", "shard"), None),
        P(("dp", "shard"), None),
        P(("dp", "shard")),
        P(),
    )
    return jax.shard_map(
        functools.partial(per_device, sizes),
        mesh=mesh,
        in_specs=placed,
        out_specs=(P(), P(), P(("dp", "shard"), None)),
        check_vma=False,
    )
```
